128 devices in a mesh: site: 32 (over y, z_lo, x), freq: 4 (over z_hi, core).
Axes of the slice: x: 4, y: 4, z: 4 (z_hi: 2, z_lo: 2; z = z_hi * 2 + z_lo), core: 2. Of those that a mesh axis runs over, the one named last changes fastest.
Arguments:
- green_tangent: float32 [128, 2, 2, 128, 512], P('site', None, None, None, 'freq'), may hold values from -6 to 6
- green_plus: float32 [128, 2, 128, 512], P('freq', None, 'site'), may hold values from -6 to 6
- green_mirror: float32 [128, 2, 128, 512], P('freq', None, 'site'), may hold values from -6 to 6
- potential: float32 [128, 2, 128, 512], P('freq', None, 'site'), may hold values from -6 to 6
- bubble: float32 [128, 2, 128, 512], P('site', None, None, 'freq'), may hold values from -0.5 to 0.5
Outputs:
- sigma_tangent: float32 [128, 2, 2, 128, 512], P('site', None, None, None, 'freq')
The draws below stay inside these ranges and needn't reach their ends.
All inputs are finite; a program needn't handle non-finite values.
Results may differ from the reference program's by a relative error of at most 0.000092.
Values sent between devices are 32-bit elements; how exact they have to be, the bound alone decides.
No kernel may reach another device: no remote copies, remote signals or barrier semaphores. Data moves between devices by JAX's collectives and lax.ppermute only.
A program may use at most 128 MiB of HBM per device.

```python
import math
import jax
import jax.numpy as jnp
from jax import lax

NX = 128
NY = 128
NF = 512
TANGENTS = 2


def levels(key, extent, cuts, least, high):
    level = 1.0
    for position, parts in cuts:
        draws = jax.random.uniform(jax.random.fold_in(jax.random.fold_in(key, 6), position), (parts,), jnp.float32, least / len(cuts), high / len(cuts))
        level = level * jnp.repeat(jnp.exp(draws), extent[position] // parts).reshape((-1,) + (1,) * (len(extent) - 1 - position))
    return level


def centred(key, shape, spread, most, cuts=(), kind=jnp.bfloat16):
    entries = spread * jax.random.normal(key, shape, jnp.float32)
    if cuts:
        entries = entries * levels(key, shape, cuts, -0.22, 0.18)
    return jnp.clip(entries, -most, most).astype(kind)


def setup_inputs(seed: int = 0) -> dict:
    seeds = jax.random.split(jax.random.key(seed), 6)
    green_tangent = centred(seeds[0], (NX, TANGENTS, 2, NY, NF), 1.0, 6.0, ((0, 32), (4, 4)), jnp.float32)
    green_plus = centred(seeds[1], (NX, 2, NY, NF), 1.0, 6.0, ((0, 4), (2, 32)), jnp.float32)
    green_mirror = centred(seeds[2], (NX, 2, NY, NF), 1.0, 6.0, ((0, 4), (2, 32)), jnp.float32)
    potential = centred(seeds[3], (NX, 2, NY, NF), 1.0, 6.0, ((0, 4), (2, 32)), jnp.float32)
    bubble = jnp.clip(jax.random.uniform(seeds[4], (NX, 2, NY, NF), jnp.float32, -0.5, 0.5) * levels(seeds[4], (NX, 2, NY, NF), ((0, 32), (3, 4)), -0.4, 0.0), -0.5, 0.5)
    return dict(green_tangent=green_tangent, green_plus=green_plus, green_mirror=green_mirror, potential=potential, bubble=bubble)


HIGHEST = lax.Precision.HIGHEST
HUBBARD = 1.0
ROWS_FORM = 'xtsyf,xk->ktsyf'
COLS_FORM = 'xtsyf,yk->xtskf'
TIME_FORM = 'xtsyf,fk->xtsyk'

def phase_table(number, factor, offset, period, sign, inward):
    indices = jnp.arange(number, dtype=jnp.int32)
    shifted = factor * indices + offset
    numerator = jnp.mod(shifted[:, None] * indices[None, :], period)
    angle = sign * 2.0 * math.pi / period * numerator.astype(jnp.float32)
    scaling = 1.0 / math.sqrt(number)
    cosine = jnp.cos(angle) * scaling
    sine = jnp.sin(angle) * scaling
    if inward:
        return (cosine, sine)
    return (cosine.T, sine.T)

def transform(source, table, form):
    cosine, sine = table
    real_part = source[:, :, :, 0]
    imag_part = source[:, :, :, 1]
    real_cos = jnp.einsum(form, real_part, cosine, precision=HIGHEST)
    real_sin = jnp.einsum(form, real_part, sine, precision=HIGHEST)
    imag_cos = jnp.einsum(form, imag_part, cosine, precision=HIGHEST)
    imag_sin = jnp.einsum(form, imag_part, sine, precision=HIGHEST)
    return jnp.stack([real_cos - imag_sin, real_sin + imag_cos], axis=3)

def complex_product(left, right):
    return jnp.stack([left[:, :, 0] * right[:, :, 0] - left[:, :, 1] * right[:, :, 1], left[:, :, 0] * right[:, :, 1] + left[:, :, 1] * right[:, :, 0]], axis=2)

def inverse_square(real_part, imag_part):
    magnitude = real_part * real_part + imag_part * imag_part
    inv_real = real_part / magnitude
    inv_imag = -imag_part / magnitude
    return (inv_real * inv_real - inv_imag * inv_imag, 2.0 * inv_real * inv_imag)

def rpa_weight(bubble):
    chi_real = HUBBARD * bubble[:, 0]
    chi_imag = HUBBARD * bubble[:, 1]
    spin_real, spin_imag = inverse_square(1.0 - chi_real, -chi_imag)
    charge_real, charge_imag = inverse_square(1.0 + chi_real, chi_imag)
    factor = HUBBARD * HUBBARD
    return jnp.stack([factor * (1.5 * spin_real + 0.5 * charge_real - 1.0), factor * (1.5 * spin_imag + 0.5 * charge_imag)], axis=1)

def three_way(source, tables):
    source = transform(source, tables[1], COLS_FORM)
    source = transform(source, tables[0], ROWS_FORM)
    return transform(source, tables[2], TIME_FORM)

def reference(green_tangent, green_plus, green_mirror, potential, bubble):
    fermion_in = (phase_table(NX, 1, 0, NX, 1.0, True), phase_table(NY, 1, 0, NY, 1.0, True), phase_table(NF, 2, 1 - NF, 2 * NF, -1.0, True))
    boson_out = (phase_table(NX, 1, 0, NX, -1.0, False), phase_table(NY, 1, 0, NY, -1.0, False), phase_table(NF, 1, -(NF // 2), NF, 1.0, False))
    boson_in = (phase_table(NX, 1, 0, NX, 1.0, True), phase_table(NY, 1, 0, NY, 1.0, True), phase_table(NF, 1, -(NF // 2), NF, -1.0, True))
    fermion_out = (phase_table(NX, 1, 0, NX, -1.0, False), phase_table(NY, 1, 0, NY, -1.0, False), phase_table(NF, 2, 1 - NF, 2 * NF, 1.0, False))
    weight = rpa_weight(bubble)
    mirror = jnp.stack([green_tangent[:, :, 0], -green_tangent[:, :, 1]], axis=2)
    paired = three_way(jnp.stack([green_tangent, mirror], axis=2), fermion_in)
    plus_part = paired[:, :, 0]
    minus_part = jnp.stack([paired[:, :, 1, 0], -paired[:, :, 1, 1]], axis=2)
    base_plus = green_plus[:, None]
    chi_change = -(complex_product(plus_part, green_mirror[:, None]) + complex_product(base_plus, minus_part))
    chi_q = three_way(chi_change[:, :, None], boson_out)[:, :, 0]
    pot_q = complex_product(weight[:, None], chi_q)
    pot_change = three_way(pot_q[:, :, None], boson_in)[:, :, 0]
    sigma_real = complex_product(potential[:, None], plus_part) + complex_product(pot_change, base_plus)
    return three_way(sigma_real[:, :, None], fermion_out)[:, :, 0]
```

```python
import math

import jax
import jax.numpy as jnp
import ml_dtypes
import numpy as np
from jax import lax
from jax.experimental import pallas as pl
from jax.experimental.pallas import tpu as pltpu
from jax.sharding import PartitionSpec as P

N = 128
NF = 512
BOTH = ("site", "freq")
CHIPS = 64
BF16 = jnp.bfloat16
F32 = jnp.float32


def column(chip, slab):
    site, z_hi = divmod(chip, 2)
    base = 4 * site + z_hi if site < 16 else 4 * (31 - site) + 2 + z_hi
    if slab == 0:
        return base
    return (N - base) % N if base else N // 2


COLUMN = np.array([[column(chip, slab) for chip in range(CHIPS)] for slab in range(2)])
HOLDER = {int(COLUMN[slab, chip]): 2 * chip + slab for chip in range(CHIPS) for slab in range(2)}


def phases(rows, cols, period, sign, number):
    turns = np.mod(np.outer(rows, cols), period)
    return np.exp(sign * 2j * math.pi / period * turns) / math.sqrt(number)


def real_form(matrix):
    return np.stack(
        [np.stack([matrix.real, -matrix.imag], 1), np.stack([matrix.imag, matrix.real], 1)]
    )


def split(table):
    table = table.astype(np.float32)
    high = table.astype(ml_dtypes.bfloat16)
    low = (table - high.astype(np.float32)).astype(ml_dtypes.bfloat16)
    return np.stack([high, low])


IDX = np.arange(N)
TIME = np.arange(NF)
FERMI = 2 * TIME + 1 - NF
BOSE = TIME - NF // 2


def y_to_columns():
    return split(real_form(phases(COLUMN.reshape(-1), IDX, N, 1, N)).reshape(256, 256))


def y_to_momenta():
    return split(real_form(phases(IDX, COLUMN.reshape(-1), N, -1, N)).reshape(256, 256))


def x_in(sign):
    return real_form(phases(IDX, IDX, N, sign, N)).transpose(0, 1, 3, 2).reshape(256, 256)


def x_in_pair():
    minus = x_in(-1).reshape(2, 128, 256) * np.array([1.0, -1.0])[:, None, None]
    return split(np.concatenate([x_in(1), minus.reshape(256, 256)]))


def x_out():
    return split(real_form(phases(IDX, IDX, N, -1, N)).transpose(1, 0, 2, 3).reshape(256, 256))


def t_in(levels, period, sign):
    table = real_form(phases(TIME, levels, period, sign, NF))
    table = table.reshape(2, 4, 128, 2, NF).transpose(3, 4, 1, 0, 2)
    return split(table.reshape(1024, 1024))


def t_out(levels, period, sign):
    table = real_form(phases(levels, TIME, period, sign, NF))
    table = table.reshape(2, NF, 2, 4, 128).transpose(3, 2, 4, 0, 1)
    return split(table.reshape(1024, 1024))


def dot(a, b):
    return lax.dot_general(a, b, (((1,), (0,)), ((), ())), preferred_element_type=F32)


def halves(value):
    high = value.astype(BF16)
    return high, (value - high.astype(F32)).astype(BF16)


def dot3(a_high, a_low, b_high, b_low):
    return dot(a_high, b_high) + (dot(a_high, b_low) + dot(a_low, b_high))


def slab_rows(core, slot, row):
    return pl.ds((core * 2 + slot) * 8 + row, CHIPS, stride=32)


def store_columns(result, core, out_ref):
    for slot in range(2):
        slab = slot ^ core
        for kx in range(4):
            for part in range(2):
                top = part * 128 + slab * CHIPS
                out_ref[slab_rows(core, slot, kx * 2 + part), :] = result[
                    top : top + CHIPS, kx * 128 : kx * 128 + 128
                ]


def load_columns(core, in_ref):
    blocks = []
    for kx in range(4):
        pieces = []
        for part in range(2):
            for slab in range(2):
                pieces.append(in_ref[slab_rows(core, slab ^ core, kx * 2 + part), :])
        blocks.append(jnp.concatenate(pieces, axis=0))
    return jnp.concatenate(blocks, axis=1)


def first_kernel(table_ref, green_ref, out_ref):
    for core in range(2):
        source = jnp.concatenate(
            [green_ref[kx, core].reshape(256, 128) for kx in range(4)], axis=1
        )
        high, low = halves(source)
        result = dot3(table_ref[0], table_ref[1], high, low)
        store_columns(result, core, out_ref)


def inverse_square(real_part, imag_part):
    scale = 1.0 / (real_part * real_part + imag_part * imag_part)
    inv_real = real_part * scale
    inv_imag = -imag_part * scale
    return (inv_real * inv_real - inv_imag * inv_imag, 2.0 * inv_real * inv_imag)


def middle_kernel(in_table_ref, out_table_ref, bubble_ref, in_ref, out_ref):
    weight_real, weight_imag = [], []
    for kx in range(4):
        chi_real = bubble_ref[kx, 0]
        chi_imag = bubble_ref[kx, 1]
        spin_real, spin_imag = inverse_square(1.0 - chi_real, -chi_imag)
        charge_real, charge_imag = inverse_square(1.0 + chi_real, chi_imag)
        weight_real.append(1.5 * spin_real + 0.5 * charge_real - 1.0)
        weight_imag.append(1.5 * spin_imag + 0.5 * charge_imag)
    weight_real = jnp.concatenate(weight_real, axis=1)
    weight_imag = jnp.concatenate(weight_imag, axis=1)
    for core in range(2):
        high, low = halves(load_columns(core, in_ref))
        chi = dot3(in_table_ref[0], in_table_ref[1], high, low)
        real, imag = chi[:128], chi[128:]
        pot = jnp.concatenate(
            [
                weight_real * real - weight_imag * imag,
                weight_real * imag + weight_imag * real,
            ],
            axis=0,
        )
        high, low = halves(pot)
        result = dot3(out_table_ref[0], out_table_ref[1], high, low)
        store_columns(result, core, out_ref)


def last_kernel(table_ref, in_ref, out_ref):
    for core in range(2):
        high, low = halves(load_columns(core, in_ref))
        result = dot3(table_ref[0], table_ref[1], high, low)
        for kx in range(4):
            for part in range(2):
                out_ref[kx, core, part] = result[
                    part * 128 : part * 128 + 128, kx * 128 : kx * 128 + 128
                ]


def place():
    site = lax.axis_index("site")
    freq = lax.axis_index("freq")
    z_hi = freq // 2
    core = lax.rem(freq, 2)
    row = jnp.where(site < 16, z_hi, 2 + z_hi)
    image = lax.rem(4 - row, 4)
    own = jnp.where(core == 0, row, image)
    other = jnp.where(core == 0, image, row)
    alone = jnp.logical_and(site == 0, z_hi == 0)
    return alone, own, other


def gather_slot(in_ref, slot):
    return jnp.concatenate(
        [in_ref[:, freq, slot].reshape(256, 128) for freq in range(4)], axis=1
    )


def beside(result):
    return jnp.concatenate([result[:128], result[128:]], axis=1)


def finish(x_out_ref, acc_ref, out_ref):
    for slot in range(2):
        top = slot * 128
        source = jnp.concatenate(
            [acc_ref[top : top + 128, :512], acc_ref[top : top + 128, 512:]], axis=0
        )
        high, low = halves(source)
        result = dot3(x_out_ref[0], x_out_ref[1], high, low)
        for freq in range(4):
            out_ref[:, freq, slot] = result[:, freq * 128 : freq * 128 + 128].reshape(32, 8, 128)


def accumulate(step, t_out_ref, work_ref, acc_ref):
    update = dot3(work_ref[0], work_ref[1], t_out_ref[0], t_out_ref[1])

    @pl.when(step == 0)
    def _():
        acc_ref[...] = update

    @pl.when(step > 0)
    def _():
        acc_ref[...] += update


def put_halves(ref, rows, value):
    high, low = halves(value)
    ref[0, rows, :] = high
    ref[1, rows, :] = low


def chi_kernel(
    x_in_ref, t_in_ref, t_out_ref, x_out_ref, in_ref,
    own0, own1, own2, own3, other0, other1, other2, other3,
    out_ref, plus_ref, left_ref, time_ref, work_ref, acc_ref,
):
    step = pl.program_id(0)
    alone, own_row, other_row = place()

    @pl.when(step == 0)
    def _():
        for slot in range(2):
            high, low = halves(gather_slot(in_ref, slot))
            result = dot3(x_in_ref[0], x_in_ref[1], high, low)
            put_halves(left_ref, pl.ds(slot * 128, 128), beside(result[:256]))
            image = jnp.where(alone, slot, 1 - slot)
            rows = pl.ds(pl.multiple_of(256 + image * 128, 128), 128)
            put_halves(left_ref, rows, beside(result[256:]))

    time_ref[...] = dot3(left_ref[0], left_ref[1], t_in_ref[0], t_in_ref[1])
    for slot, row, pieces in (
        (0, own_row, (own0, own1, own2, own3)),
        (1, other_row, (other0, other1, other2, other3)),
    ):
        for shift, piece in enumerate(pieces):
            block = lax.rem(row - shift + 4, 4)
            start = pl.multiple_of(slot * 128 + block * 32, 32)
            rows = pl.ds(start, 32)
            plus = time_ref[rows, :]
            minus = time_ref[pl.ds(256 + start, 32), :]
            plus_real, plus_imag = plus[:, :128], plus[:, 128:]
            minus_real, minus_imag = minus[:, :128], -minus[:, 128:]
            base_real, base_imag = piece[0, 0], piece[0, 1]
            mirror_real, mirror_imag = piece[1, 0], piece[1, 1]
            chi_real = (
                plus_real * mirror_real - plus_imag * mirror_imag
                + base_real * minus_real - base_imag * minus_imag
            )
            chi_imag = (
                plus_real * mirror_imag + plus_imag * mirror_real
                + base_real * minus_imag + base_imag * minus_real
            )
            put_halves(work_ref, rows, -jnp.concatenate([chi_real, chi_imag], axis=1))
            plus_ref[rows, :] = plus
    accumulate(step, t_out_ref, work_ref, acc_ref)

    @pl.when(step == 3)
    def _():
        finish(x_out_ref, acc_ref, out_ref)


def sigma_kernel(
    x_in_ref, t_in_ref, t_out_ref, x_out_ref, in_ref, plus_ref,
    own0, own1, own2, own3, other0, other1, other2, other3,
    out_ref, left_ref, time_ref, work_ref, acc_ref,
):
    step = pl.program_id(0)
    _, own_row, other_row = place()

    @pl.when(step == 0)
    def _():
        for slot in range(2):
            high, low = halves(gather_slot(in_ref, slot))
            result = dot3(x_in_ref[0], x_in_ref[1], high, low)
            put_halves(left_ref, pl.ds(slot * 128, 128), beside(result))

    time_ref[...] = dot3(left_ref[0], left_ref[1], t_in_ref[0], t_in_ref[1])
    for slot, row, pieces in (
        (0, own_row, (own0, own1, own2, own3)),
        (1, other_row, (other0, other1, other2, other3)),
    ):
        for shift, piece in enumerate(pieces):
            block = lax.rem(row - shift + 4, 4)
            rows = pl.ds(pl.multiple_of(slot * 128 + block * 32, 32), 32)
            change = time_ref[rows, :]
            plus = plus_ref[rows, :]
            change_real, change_imag = change[:, :128], change[:, 128:]
            plus_real, plus_imag = plus[:, :128], plus[:, 128:]
            base_real, base_imag = piece[0, 0], piece[0, 1]
            pot_real, pot_imag = piece[2, 0], piece[2, 1]
            real = (
                pot_real * plus_real - pot_imag * plus_imag
                + change_real * base_real - change_imag * base_imag
            )
            imag = (
                pot_real * plus_imag + pot_imag * plus_real
                + change_real * base_imag + change_imag * base_real
            )
            put_halves(work_ref, rows, jnp.concatenate([real, imag], axis=1))
    accumulate(step, t_out_ref, work_ref, acc_ref)

    @pl.when(step == 3)
    def _():
        finish(x_out_ref, acc_ref, out_ref)


PARAMS = pltpu.CompilerParams(vmem_limit_bytes=40 * 1024 * 1024)


def simple_call(body, name, out_shape, flops, *operands):
    size = sum(operand.size * operand.dtype.itemsize for operand in operands)
    return pl.pallas_call(
        body,
        out_shape=jax.ShapeDtypeStruct(out_shape, F32),
        compiler_params=PARAMS,
        cost_estimate=pl.CostEstimate(
            flops=flops, bytes_accessed=size + 4 * math.prod(out_shape), transcendentals=0
        ),
        name=name,
    )(*operands)


def whole(shape):
    return pl.BlockSpec(shape, lambda step: (0,) * len(shape))


def real_space_call(body, name, tables, source, plus, pieces):
    x_table, t_table, t_back, x_back = tables
    wide = x_table.shape[1]
    piece_spec = pl.BlockSpec((3, 2, 32, 128), lambda step: (0, 0, 0, step))
    plus_spec = pl.BlockSpec((256, 256), lambda step: (0, step))
    in_specs = [
        whole((2, wide, 256)),
        pl.BlockSpec((2, 1024, 256), lambda step: (0, 0, step)),
        pl.BlockSpec((2, 256, 1024), lambda step: (0, step, 0)),
        whole((2, 256, 256)),
        whole((32, 4, 2, 8, 128)),
    ]
    operands = [x_table, t_table, t_back, x_back, source.reshape(32, 4, 2, 8, 128)]
    out_shape = [jax.ShapeDtypeStruct((32, 4, 2, 8, 128), F32)]
    out_specs = [whole((32, 4, 2, 8, 128))]
    if plus is None:
        out_shape.append(jax.ShapeDtypeStruct((256, 1024), F32))
        out_specs.append(plus_spec)
    else:
        in_specs.append(plus_spec)
        operands.append(plus)
    return pl.pallas_call(
        body,
        grid=(4,),
        in_specs=in_specs + [piece_spec] * 8,
        out_specs=out_specs,
        out_shape=out_shape,
        scratch_shapes=[
            pltpu.VMEM((2, wide, 1024), BF16),
            pltpu.VMEM((wide, 256), F32),
            pltpu.VMEM((2, 256, 256), BF16),
            pltpu.VMEM((256, 1024), F32),
        ],
        compiler_params=PARAMS,
        cost_estimate=pl.CostEstimate(
            flops=6 * 1024 * 1024 * (wide + 256), bytes_accessed=12 << 20, transcendentals=0
        ),
        name=name,
    )(*operands, *pieces)


def exchange(source):
    source = source.reshape(128, 16, 128)
    return lax.all_to_all(source, BOTH, split_axis=0, concat_axis=0, tiled=True)


def move_pieces(arrays):
    freq = lax.axis_index("freq")
    stacked = jnp.stack([array.transpose(2, 1, 0, 3) for array in arrays], axis=1)
    own, other = [], []
    for shift in range(4):
        row = lax.rem(freq + shift, 4)
        piece = lax.dynamic_index_in_dim(stacked, row, 0, keepdims=False)
        routes = [
            (4 * site + f, HOLDER[4 * site + (f + shift) % 4]) for site in range(32) for f in range(4)
        ]
        own.append(lax.ppermute(piece, BOTH, routes))
    for piece in own:
        other.append(lax.ppermute(piece, BOTH, [(n, n ^ 1) for n in range(128)]))
    return own + other


def local(green_tangent, green_plus, green_mirror, potential, bubble):
    pieces = move_pieces([green_plus, green_mirror, potential])
    columns, momenta = jnp.asarray(y_to_columns()), jnp.asarray(y_to_momenta())
    back = jnp.asarray(x_out())
    chi_tables = (
        jnp.asarray(x_in_pair()),
        jnp.asarray(t_in(FERMI, 2 * NF, -1)),
        jnp.asarray(t_out(BOSE, NF, 1)),
        back,
    )
    sigma_tables = (
        jnp.asarray(split(x_in(1))),
        jnp.asarray(t_in(BOSE, NF, -1)),
        jnp.asarray(t_out(FERMI, 2 * NF, 1)),
        back,
    )
    flops = 2 * 3 * 256 * 256 * 1024
    sent = simple_call(first_kernel, "first", (2048, 128), flops, columns, green_tangent)
    held = exchange(sent)
    sent, plus = real_space_call(chi_kernel, "chi", chi_tables, held, None, pieces)
    held = exchange(sent).reshape(2048, 128)
    sent = simple_call(middle_kernel, "middle", (2048, 128), 2 * flops, momenta, columns, bubble, held)
    held = exchange(sent)
    (sent,) = real_space_call(sigma_kernel, "sigma", sigma_tables, held, plus, pieces)
    held = exchange(sent).reshape(2048, 128)
    return simple_call(last_kernel, "last", (4, 2, 2, 128, 128), flops, momenta, held)


def solution(mesh):
    in_specs = (
        P("site", None, None, None, "freq"),
        P("freq", None, "site", None),
        P("freq", None, "site", None),
        P("freq", None, "site", None),
        P("site", None, None, "freq"),
    )
    out_specs = P("site", None, None, None, "freq")
    return jax.shard_map(local, mesh=mesh, in_specs=in_specs, out_specs=out_specs, check_vma=False)
```

```python
import math

import jax
import jax.numpy as jnp
import ml_dtypes
import numpy as np
from jax import lax
from jax.experimental import pallas as pl
from jax.experimental.pallas import tpu as pltpu
from jax.sharding import PartitionSpec as P

N = 128
NF = 512
BOTH = ("site", "freq")
CHIPS = 64
BF16 = jnp.bfloat16
F32 = jnp.float32


def column(chip, slab):
    site, z_hi = divmod(chip, 2)
    own = 4 * site + (z_hi if site < 16 else 2 - z_hi)
    if slab == 0:
        return own
    return (N - own) % N if own else N // 2


COLUMN = np.array([[column(chip, slab) for chip in range(CHIPS)] for slab in range(2)])


def routes(shift):
    pairs = []
    for chip in range(CHIPS):
        source = int(COLUMN[shift // 2, chip]) // 4 * 2 + (chip % 2 ^ shift % 2)
        pairs += [(2 * source + core, 2 * chip + core) for core in range(2)]
    return pairs


def phases(rows, cols, period, sign, number):
    turns = np.mod(np.outer(rows, cols), period)
    return np.exp(sign * 2j * math.pi / period * turns) / math.sqrt(number)


def real_form(matrix):
    return np.stack(
        [np.stack([matrix.real, -matrix.imag], 1), np.stack([matrix.imag, matrix.real], 1)]
    )


def split(table):
    table = table.astype(np.float32)
    high = table.astype(ml_dtypes.bfloat16)
    low = (table - high.astype(np.float32)).astype(ml_dtypes.bfloat16)
    return np.stack([high, low])


IDX = np.arange(N)
FERMI = (1 - NF) / 2
BOSE = -(NF // 2)


def y_to_columns():
    return split(real_form(phases(COLUMN.reshape(-1), IDX, N, 1, N)).reshape(256, 256))


def y_to_momenta():
    return split(real_form(phases(IDX, COLUMN.reshape(-1), N, -1, N)).reshape(256, 256))


def x_in(sign):
    return real_form(phases(IDX, IDX, N, sign, N)).transpose(0, 1, 3, 2).reshape(256, 256)


def x_in_pair():
    minus = x_in(-1).reshape(2, 128, 256) * np.array([1.0, -1.0])[:, None, None]
    return split(np.concatenate([x_in(1), minus.reshape(256, 256)]))


def x_out():
    return split(real_form(phases(IDX, IDX, N, -1, N)).transpose(1, 0, 2, 3).reshape(256, 256))


def t_phases(offset, sign, step):
    times = 4 * IDX + step
    return phases((IDX + offset), times, NF, sign, NF)


def t_in(offset, sign):
    tables = [real_form(t_phases(offset, sign, c).T).reshape(256, 256).T for c in range(4)]
    return split(np.stack(tables)).transpose(1, 0, 2, 3)


def t_out(offset, sign):
    tables = [real_form(t_phases(offset, sign, c)).reshape(256, 256).T for c in range(4)]
    return split(np.stack(tables)).transpose(1, 0, 2, 3)


def t_order():
    order = np.zeros((NF, NF), np.float32)
    place = np.arange(NF)
    order[4 * (place % N) + place // N, place] = 1
    return order.astype(ml_dtypes.bfloat16)


def dot(a, b):
    return lax.dot_general(a, b, (((1,), (0,)), ((), ())), preferred_element_type=F32)


def halves(value):
    high = value.astype(BF16)
    return high, (value - high.astype(F32)).astype(BF16)


def dot3(a_high, a_low, b_high, b_low):
    return dot(a_high, b_high) + (dot(a_high, b_low) + dot(a_low, b_high))


def slab_rows(core, slab, row):
    return pl.ds((core * 2 + slab) * 8 + row, CHIPS, stride=32)


def store_columns(result, core, out_ref):
    for slab in range(2):
        for kx in range(4):
            for part in range(2):
                top = part * 128 + slab * CHIPS
                out_ref[slab_rows(core, slab, kx * 2 + part), :] = result[
                    top : top + CHIPS, kx * 128 : kx * 128 + 128
                ]


def load_columns(core, in_ref):
    blocks = []
    for kx in range(4):
        pieces = []
        for part in range(2):
            for slab in range(2):
                pieces.append(in_ref[slab_rows(core, slab, kx * 2 + part), :])
        blocks.append(jnp.concatenate(pieces, axis=0))
    return jnp.concatenate(blocks, axis=1)


def fetch(source, target, sem):
    copy = pltpu.make_async_copy(source, target, sem)
    copy.start()
    return copy.wait


def first_kernel(table_hbm, green_hbm, out_ref, table_ref, green_ref, sems):
    table_here = fetch(table_hbm, table_ref, sems.at[0])
    green_here = [
        fetch(green_hbm.at[:, tangent], green_ref.at[tangent], sems.at[1 + tangent])
        for tangent in range(2)
    ]
    for tangent in range(2):
        green_here[tangent]()
        source = jnp.concatenate(
            [green_ref[tangent, kx].reshape(256, 128) for kx in range(4)], axis=1
        )
        high, low = halves(source)
        if tangent == 0:
            table_here()
        result = dot3(table_ref[0], table_ref[1], high, low)
        store_columns(result, tangent, out_ref)


def inverse_square(real_part, imag_part):
    scale = 1.0 / (real_part * real_part + imag_part * imag_part)
    inv_real = real_part * scale
    inv_imag = -imag_part * scale
    return (inv_real * inv_real - inv_imag * inv_imag, 2.0 * inv_real * inv_imag)


def middle_kernel(
    in_table_hbm, out_table_hbm, bubble_hbm, in_ref, out_ref,
    in_table_ref, out_table_ref, bubble_ref, sems,
):
    bubble_here = fetch(bubble_hbm, bubble_ref, sems.at[0])
    in_table_here = fetch(in_table_hbm, in_table_ref, sems.at[1])
    out_table_here = fetch(out_table_hbm, out_table_ref, sems.at[2])
    columns = [halves(load_columns(core, in_ref)) for core in range(2)]
    bubble_here()
    weight_real, weight_imag = [], []
    for kx in range(4):
        chi_real = bubble_ref[kx, 0]
        chi_imag = bubble_ref[kx, 1]
        spin_real, spin_imag = inverse_square(1.0 - chi_real, -chi_imag)
        charge_real, charge_imag = inverse_square(1.0 + chi_real, chi_imag)
        weight_real.append(1.5 * spin_real + 0.5 * charge_real - 1.0)
        weight_imag.append(1.5 * spin_imag + 0.5 * charge_imag)
    weight_real = jnp.concatenate(weight_real, axis=1)
    weight_imag = jnp.concatenate(weight_imag, axis=1)
    for core in range(2):
        high, low = columns[core]
        if core == 0:
            in_table_here()
        chi = dot3(in_table_ref[0], in_table_ref[1], high, low)
        real, imag = chi[:128], chi[128:]
        pot = jnp.concatenate(
            [
                weight_real * real - weight_imag * imag,
                weight_real * imag + weight_imag * real,
            ],
            axis=0,
        )
        high, low = halves(pot)
        if core == 0:
            out_table_here()
        result = dot3(out_table_ref[0], out_table_ref[1], high, low)
        store_columns(result, core, out_ref)


def last_kernel(table_hbm, in_ref, out_hbm, table_ref, out_ref, sems):
    table_here = fetch(table_hbm, table_ref, sems.at[0])
    sent = []
    for core in range(2):
        high, low = halves(load_columns(core, in_ref))
        if core == 0:
            table_here()
        result = dot3(table_ref[0], table_ref[1], high, low)
        for kx in range(4):
            for part in range(2):
                out_ref[core, kx, part] = result[
                    part * 128 : part * 128 + 128, kx * 128 : kx * 128 + 128
                ]
        sent.append(fetch(out_ref.at[core], out_hbm.at[:, core], sems.at[1 + core]))
    for gone in sent:
        gone()


def place_of(place):
    freq = lax.axis_index("freq")
    shift, swapped = place % 4, place // 4
    return shift // 2, lax.bitwise_xor(freq, 2 * (shift % 2) + swapped)


def gather_slab(in_ref, slot):
    return jnp.concatenate(
        [in_ref[:, freq, slot].reshape(256, 128) for freq in range(4)], axis=1
    )


def turned(real, imag, quarter):
    return ((real, imag), (-imag, real), (-real, -imag), (imag, -real))[quarter % 4]


def to_left(result, rows, left_ref):
    for high in range(4):
        lanes = slice(high * 128, high * 128 + 128)
        left_ref[high, rows, :] = jnp.concatenate(
            [result[:128, lanes], result[128:, lanes]], axis=1
        )


def to_times(step, left_ref, t_in_ref, sign):
    real, imag = left_ref[0, :, :128], left_ref[0, :, 128:]
    for high in range(1, 4):
        more = turned(left_ref[high, :, :128], left_ref[high, :, 128:], sign * high * step)
        real, imag = real + more[0], imag + more[1]
    first, second = halves(jnp.concatenate([real, imag], axis=1))
    return dot3(first, second, t_in_ref[step, 0], t_in_ref[step, 1])


def finish(x_out_ref, acc_ref, out_ref):
    for slab in range(2):
        rows = slice(slab * 128, slab * 128 + 128)
        source = jnp.concatenate(
            [
                jnp.concatenate([acc_ref[high, rows, :128] for high in range(4)], axis=1),
                jnp.concatenate([acc_ref[high, rows, 128:] for high in range(4)], axis=1),
            ],
            axis=0,
        )
        high, low = halves(source)
        result = dot3(x_out_ref[0], x_out_ref[1], high, low)
        for freq in range(4):
            out_ref[:, freq, slab] = result[:, freq * 128 : freq * 128 + 128].reshape(32, 8, 128)


def accumulate(step, first, second, t_out_ref, acc_ref):
    update = dot3(first, second, t_out_ref[step, 0], t_out_ref[step, 1])
    real, imag = update[:, :128], update[:, 128:]
    for high in range(4):
        if step:
            acc_ref[high] += jnp.concatenate(turned(real, imag, high * step), axis=1)
        else:
            acc_ref[high] = update


def prepare_kernel(order_hbm, *refs):
    pieces, (out_hbm, order_ref, out_ref, sems) = refs[:8], refs[8:]
    order_here = fetch(order_hbm, order_ref, sems.at[0])
    for place, ref in enumerate(pieces):
        arrays = ref.shape[0]
        value = ref[...].reshape(arrays * 64, NF)
        first = value.astype(BF16)
        rest = value - first.astype(F32)
        second, third = halves(rest)
        if place == 0:
            order_here()
        order = order_ref[...]
        moved = (dot(first, order) + dot(second, order)) + dot(third, order)
        slab, block = place_of(place)
        rows = pl.ds(pl.multiple_of(slab * 128 + block * 32, 32), 32)
        for array in range(arrays):
            for part in range(2):
                top = (array * 2 + part) * 32
                out_ref[array, part, rows, :] = moved[top : top + 32]
    fetch(out_ref, out_hbm, sems.at[1])()


def time_lanes(step, width):
    return pl.ds(step * width, width)


def fetch_fields(field_hbm, field_ref, sems):
    return [
        fetch(
            field_hbm.at[pl.ds(0, field_ref.shape[0]), :, :, time_lanes(step, 128)],
            field_ref.at[:, :, :, time_lanes(step, 128)],
            sems.at[step],
        )
        for step in range(4)
    ]


def fetch_tables(hbm_refs, refs, sems):
    return [fetch(hbm, ref, sems.at[place]) for place, (hbm, ref) in enumerate(zip(hbm_refs, refs))]


def chi_kernel(*refs):
    tables_hbm, in_ref, base_hbm, out_ref, plus_hbm = refs[:4], *refs[4:8]
    tables, (base_ref, plus_ref, left_ref, acc_ref, sems, base_sems, plus_sems) = refs[8:12], refs[12:]
    x_in_ref, t_in_ref, t_out_ref, x_out_ref = tables
    x_in_here, t_in_here, t_out_here, x_out_here = fetch_tables(tables_hbm, tables, sems)
    base_here = fetch_fields(base_hbm, base_ref, base_sems)
    site, freq = lax.axis_index("site"), lax.axis_index("freq")
    alone = jnp.logical_and(site == 0, freq < 2)

    for slab in range(2):
        high, low = halves(gather_slab(in_ref, slab))
        if slab == 0:
            x_in_here()
        result = dot3(x_in_ref[0], x_in_ref[1], high, low)
        to_left(result[:256], pl.ds(slab * 128, 128), left_ref)
        image = jnp.where(alone, slab, 1 - slab)
        rows = pl.ds(pl.multiple_of(256 + image * 128, 128), 128)
        to_left(result[256:], rows, left_ref)

    t_in_here()
    plus_gone = []
    for step in range(4):
        times = to_times(step, left_ref, t_in_ref, -1)
        plus, minus = times[:256], times[256:]
        lanes = time_lanes(step, 256)
        plus_ref[:, lanes] = plus
        plus_gone.append(fetch(plus_ref.at[:, lanes], plus_hbm.at[:, lanes], plus_sems.at[step]))
        plus_real, plus_imag = plus[:, :128], plus[:, 128:]
        minus_real, minus_imag = minus[:, :128], -minus[:, 128:]
        base_here[step]()
        block = time_lanes(step, 128)
        base_real, base_imag = base_ref[0, 0, :, block], base_ref[0, 1, :, block]
        mirror_real, mirror_imag = base_ref[1, 0, :, block], base_ref[1, 1, :, block]
        chi_real = (
            plus_real * mirror_real - plus_imag * mirror_imag
            + base_real * minus_real - base_imag * minus_imag
        )
        chi_imag = (
            plus_real * mirror_imag + plus_imag * mirror_real
            + base_real * minus_imag + base_imag * minus_real
        )
        first, second = halves(-jnp.concatenate([chi_real, chi_imag], axis=1))
        if step == 0:
            t_out_here()
        accumulate(step, first, second, t_out_ref, acc_ref)
    x_out_here()
    finish(x_out_ref, acc_ref, out_ref)
    for gone in plus_gone:
        gone()


def sigma_kernel(*refs):
    tables_hbm, (in_ref, base_hbm, pot_hbm, plus_hbm, out_ref) = refs[:4], refs[4:9]
    tables, refs = refs[9:13], refs[13:]
    base_ref, pot_ref, plus_ref, left_ref, acc_ref, sems, base_sems, pot_sems, plus_sem = refs
    x_in_ref, t_in_ref, t_out_ref, x_out_ref = tables
    x_in_here, t_in_here, t_out_here, x_out_here = fetch_tables(tables_hbm, tables, sems)
    plus_here = fetch(plus_hbm, plus_ref, plus_sem.at[0])
    base_here = fetch_fields(base_hbm, base_ref, base_sems)
    pot_here = fetch_fields(pot_hbm, pot_ref, pot_sems)

    for slab in range(2):
        high, low = halves(gather_slab(in_ref, slab))
        if slab == 0:
            x_in_here()
        result = dot3(x_in_ref[0], x_in_ref[1], high, low)
        to_left(result, pl.ds(slab * 128, 128), left_ref)

    t_in_here()
    for step in range(4):
        change = to_times(step, left_ref, t_in_ref, -1)
        if step == 0:
            plus_here()
        base_here[step]()
        pot_here[step]()
        plus = plus_ref[:, time_lanes(step, 256)]
        block = time_lanes(step, 128)
        change_real, change_imag = change[:, :128], change[:, 128:]
        plus_real, plus_imag = plus[:, :128], plus[:, 128:]
        base_real, base_imag = base_ref[0, 0, :, block], base_ref[0, 1, :, block]
        pot_real, pot_imag = pot_ref[0, 0, :, block], pot_ref[0, 1, :, block]
        real = (
            pot_real * plus_real - pot_imag * plus_imag
            + change_real * base_real - change_imag * base_imag
        )
        imag = (
            pot_real * plus_imag + pot_imag * plus_real
            + change_real * base_imag + change_imag * base_real
        )
        first, second = halves(jnp.concatenate([real, imag], axis=1))
        if step == 0:
            t_out_here()
        accumulate(step, first, second, t_out_ref, acc_ref)
    x_out_here()
    finish(x_out_ref, acc_ref, out_ref)


PARAMS = pltpu.CompilerParams(vmem_limit_bytes=24 * 1024 * 1024)
WORK = 3 << 31
HBM = pl.BlockSpec(memory_space=pltpu.HBM)
HERE = pl.BlockSpec(memory_space=pltpu.VMEM)


def call(body, name, in_specs, out_specs, out_shape, scratch, flops, *operands):
    size = sum(operand.size * operand.dtype.itemsize for operand in operands)
    return pl.pallas_call(
        body,
        in_specs=in_specs,
        out_specs=out_specs,
        out_shape=[
            pltpu.HBM(shape, F32) if spec is HBM else jax.ShapeDtypeStruct(shape, F32)
            for shape, spec in zip(out_shape, out_specs)
        ],
        scratch_shapes=scratch,
        compiler_params=PARAMS,
        cost_estimate=pl.CostEstimate(flops=flops, bytes_accessed=size, transcendentals=0),
        name=name,
    )(*[
        pltpu.with_memory_space_constraint(operand, pltpu.HBM) if spec is HBM else operand
        for operand, spec in zip(operands, in_specs)
    ])


def like(array):
    return pltpu.VMEM(array.shape, array.dtype)


def sems(number):
    return pltpu.SemaphoreType.DMA((number,))


SLABS = (32, 4, 2, 8, 128)
TURN = 2 * 3 * 256 * 256 * 1024


def first_call(table, green):
    scratch = [like(table), pltpu.VMEM((2, 4, 2, 128, 128), F32), sems(3)]
    return call(
        first_kernel, "first", [HBM, HBM], [HERE], [(2048, 128)], scratch, TURN, table, green
    )[0]


def middle_call(momenta, columns, bubble, held):
    scratch = [like(momenta), like(columns), like(bubble), sems(3)]
    return call(
        middle_kernel, "middle", [HBM, HBM, HBM, HERE], [HERE], [(2048, 128)], scratch, 2 * TURN,
        momenta, columns, bubble, held,
    )[0]


def last_call(table, held):
    shape = (4, 2, 2, 128, 128)
    scratch = [like(table), pltpu.VMEM((2, 4, 2, 128, 128), F32), sems(3)]
    return call(last_kernel, "last", [HBM, HERE], [HBM], [shape], scratch, TURN, table, held)[0]


def prepare_call(pieces):
    shape = (pieces[0].shape[0], 2, 256, NF)
    order = jnp.asarray(t_order())
    scratch = [like(order), pltpu.VMEM(shape, F32), sems(2)]
    return call(
        prepare_kernel, "prepare", [HBM] + [HERE] * 8, [HBM], [shape], scratch, WORK, order, *pieces
    )[0]


def field(arrays):
    return pltpu.VMEM((arrays, 2, 256, NF), F32)


PLUS = (256, 1024)


def chi_call(tables, held, base):
    scratch = [
        *map(like, tables), field(2), pltpu.VMEM(PLUS, F32), pltpu.VMEM((4, 512, 256), F32),
        pltpu.VMEM((4, 256, 256), F32), sems(4), sems(4), sems(4),
    ]
    return call(
        chi_kernel, "chi", [HBM] * 4 + [HERE, HBM], [HERE, HBM], [SLABS, PLUS], scratch, 7 * TURN,
        *tables, held.reshape(SLABS), base,
    )


def sigma_call(tables, held, base, pot, plus):
    scratch = [
        *map(like, tables), field(1), field(1), pltpu.VMEM(PLUS, F32),
        pltpu.VMEM((4, 256, 256), F32), pltpu.VMEM((4, 256, 256), F32), sems(4), sems(4), sems(4), sems(1),
    ]
    return call(
        sigma_kernel, "sigma", [HBM] * 4 + [HERE, HBM, HBM, HBM], [HERE], [SLABS], scratch, 4 * TURN,
        *tables, held.reshape(SLABS), base, pot, plus,
    )[0]


def exchange(source):
    source = source.reshape(128, 16, 128)
    return lax.all_to_all(source, BOTH, split_axis=0, concat_axis=0, tiled=True)


def pack(arrays):
    site, freq = lax.axis_index("site"), lax.axis_index("freq")
    z_hi = freq // 2
    low = (z_hi, 1 - z_hi, 2 + z_hi, 3 - z_hi)
    high = (2 - z_hi, 1 + z_hi, 3 * z_hi, 3 - 3 * z_hi)
    stacked = jnp.stack([array.transpose(2, 1, 0, 3) for array in arrays], axis=1)
    return [
        lax.dynamic_index_in_dim(stacked, jnp.where(site < 16, low[k], high[k]), 0, keepdims=False)
        for k in range(4)
    ]


def send(rows):
    return [rows[0]] + [lax.ppermute(rows[shift], BOTH, routes(shift)) for shift in (1, 2, 3)]


def both_cores(own):
    return own + [lax.ppermute(piece, "freq", [(f, f ^ 1) for f in range(4)]) for piece in own]


def local(green_tangent, green_plus, green_mirror, potential, bubble):
    base = prepare_call(both_cores(send(pack([green_plus, green_mirror]))))
    columns, momenta = jnp.asarray(y_to_columns()), jnp.asarray(y_to_momenta())
    back = jnp.asarray(x_out())
    chi_tables = (
        jnp.asarray(x_in_pair()), jnp.asarray(t_in(FERMI, -1)), jnp.asarray(t_out(BOSE, 1)), back
    )
    sigma_tables = (
        jnp.asarray(split(x_in(1))), jnp.asarray(t_in(BOSE, -1)), jnp.asarray(t_out(FERMI, 1)), back
    )
    sent = first_call(columns, green_tangent)
    potential, sent = lax.optimization_barrier((potential, sent))
    held = exchange(sent)
    sent, plus = chi_call(chi_tables, held, base)
    potential, sent = lax.optimization_barrier((potential, sent))
    own = send(pack([potential]))
    held = exchange(sent).reshape(2048, 128)
    sent = middle_call(momenta, columns, bubble, held)
    own, sent = lax.optimization_barrier((own, sent))
    pot = prepare_call(both_cores(own))
    held = exchange(sent)
    sent = sigma_call(sigma_tables, held, base, pot, plus)
    held = exchange(sent).reshape(2048, 128)
    return last_call(momenta, held)


def solution(mesh):
    in_specs = (
        P("site", None, None, None, "freq"),
        P("freq", None, "site", None),
        P("freq", None, "site", None),
        P("freq", None, "site", None),
        P("site", None, None, "freq"),
    )
    out_specs = P("site", None, None, None, "freq")
    return jax.shard_map(local, mesh=mesh, in_specs=in_specs, out_specs=out_specs, check_vma=False)
```

```python
import math

import jax
import jax.numpy as jnp
import ml_dtypes
import numpy as np
from jax import lax
from jax.experimental import pallas as pl
from jax.experimental.pallas import tpu as pltpu
from jax.sharding import PartitionSpec as P

N = 128
NF = 512
BOTH = ("site", "freq")
CHIPS = 64
BF16 = jnp.bfloat16
F32 = jnp.float32


def column(chip, slab):
    site, z_hi = divmod(chip, 2)
    own = 4 * site + (z_hi if site < 16 else 2 - z_hi)
    if slab == 0:
        return own
    return (N - own) % N if own else N // 2


COLUMN = np.array([[column(chip, slab) for chip in range(CHIPS)] for slab in range(2)])


def routes(shift):
    pairs = []
    for chip in range(CHIPS):
        source = int(COLUMN[shift // 2, chip]) // 4 * 2 + (chip % 2 ^ shift % 2)
        pairs += [(2 * source + core, 2 * chip + core) for core in range(2)]
    return pairs


def phases(rows, cols, period, sign, number):
    turns = np.mod(np.outer(rows, cols), period)
    return np.exp(sign * 2j * math.pi / period * turns) / math.sqrt(number)


def real_form(matrix):
    return np.stack(
        [np.stack([matrix.real, -matrix.imag], 1), np.stack([matrix.imag, matrix.real], 1)]
    )


def split(table):
    table = table.astype(np.float32)
    high = table.astype(ml_dtypes.bfloat16)
    low = (table - high.astype(np.float32)).astype(ml_dtypes.bfloat16)
    return np.stack([high, low])


IDX = np.arange(N)
FERMI = (1 - NF) / 2
BOSE = -(NF // 2)


def y_to_columns():
    return split(real_form(phases(COLUMN.reshape(-1), IDX, N, 1, N)).reshape(256, 256))


def y_to_momenta():
    return split(real_form(phases(IDX, COLUMN.reshape(-1), N, -1, N)).reshape(256, 256))


def x_in(sign):
    return real_form(phases(IDX, IDX, N, sign, N)).transpose(0, 1, 3, 2).reshape(256, 256)


def x_out():
    return split(real_form(phases(IDX, IDX, N, -1, N)).transpose(1, 0, 2, 3).reshape(256, 256))


def t_phases(offset, sign, step):
    times = 4 * IDX + step
    return phases((IDX + offset), times, NF, sign, NF)


def t_in(offset, sign):
    tables = [real_form(t_phases(offset, sign, c).T).reshape(256, 256).T for c in range(4)]
    return split(np.stack(tables)).transpose(1, 0, 2, 3)


def t_out(offset, sign):
    tables = [real_form(t_phases(offset, sign, c)).reshape(256, 256).T for c in range(4)]
    return split(np.stack(tables)).transpose(1, 0, 2, 3)


def t_order():
    order = np.zeros((NF, NF), np.float32)
    place = np.arange(NF)
    order[4 * (place % N) + place // N, place] = 1
    return order.astype(ml_dtypes.bfloat16)


def dot(a, b):
    return lax.dot_general(a, b, (((1,), (0,)), ((), ())), preferred_element_type=F32)


def halves(value):
    high = value.astype(BF16)
    return high, (value - high.astype(F32)).astype(BF16)


def dot3(a_high, a_low, b_high, b_low):
    return dot(a_high, b_high) + (dot(a_high, b_low) + dot(a_low, b_high))


def slab_rows(core, slab, row):
    return pl.ds((core * 2 + slab) * 8 + row, CHIPS, stride=32)


def store_columns(result, core, out_ref):
    for slab in range(2):
        for kx in range(4):
            for part in range(2):
                top = part * 128 + slab * CHIPS
                out_ref[slab_rows(core, slab, kx * 2 + part), :] = result[
                    top : top + CHIPS, kx * 128 : kx * 128 + 128
                ]


def load_columns(core, in_ref):
    blocks = []
    for kx in range(4):
        pieces = []
        for part in range(2):
            for slab in range(2):
                pieces.append(in_ref[slab_rows(core, slab, kx * 2 + part), :])
        blocks.append(jnp.concatenate(pieces, axis=0))
    return jnp.concatenate(blocks, axis=1)


def fetch(source, target, sem):
    copy = pltpu.make_async_copy(source, target, sem)
    copy.start()
    return copy.wait


def leave(core, out_ref, out_hbm, sems):
    share = pl.ds(core * 16, 16)
    return fetch(out_ref.reshape(CHIPS, 32, 128).at[:, share], out_hbm.at[:, share], sems.at[3 + core])


def sort_rows(sources, outs, sems):
    site, freq = lax.axis_index("site"), lax.axis_index("freq")
    z_hi = freq // 2
    low = (z_hi, 1 - z_hi, 2 + z_hi, 3 - z_hi)
    high = (2 - z_hi, 1 + z_hi, 3 * z_hi, 3 - 3 * z_hi)
    gone = []
    for shift in (1, 2, 3, 0):
        row = jnp.where(site < 16, low[shift], high[shift])
        for array, source in enumerate(sources):
            sem = sems.at[shift * len(sources) + array]
            gone.append(fetch(source.at[:, :, row], outs[shift].at[array], sem))
    return gone


def pack_kernel(source, out0, out1, out2, out3, sems):
    for wait in sort_rows((source,), (out0, out1, out2, out3), sems):
        wait()


def begin_kernel(
    plus_hbm, mirror_hbm, table_hbm, green_hbm, out0, out1, out2, out3, out_hbm,
    table_ref, green_ref, out_ref, row_sems, sems,
):
    rows_gone = sort_rows((plus_hbm, mirror_hbm), (out0, out1, out2, out3), row_sems)
    green_here = []
    for tangent in range(2):
        green_here.append(
            fetch(green_hbm.at[:, tangent], green_ref.at[tangent], sems.at[1 + tangent])
        )
        if tangent == 0:
            table_here = fetch(table_hbm, table_ref, sems.at[0])
    left = []
    for tangent in range(2):
        green_here[tangent]()
        source = jnp.concatenate(
            [green_ref[tangent, kx].reshape(256, 128) for kx in range(4)], axis=1
        )
        high, low = halves(source)
        if tangent == 0:
            table_here()
        result = dot3(table_ref[0], table_ref[1], high, low)
        store_columns(result, tangent, out_ref)
        left.append(leave(tangent, out_ref, out_hbm, sems))
    for wait in rows_gone + left:
        wait()


def inverse_square(real_part, imag_part):
    scale = 1.0 / (real_part * real_part + imag_part * imag_part)
    inv_real = real_part * scale
    inv_imag = -imag_part * scale
    return (inv_real * inv_real - inv_imag * inv_imag, 2.0 * inv_real * inv_imag)


def weight_kernel(bubble_ref, table_hbm, weight_hbm, table_ref, weight_ref, sems):
    table_here = fetch(table_hbm, table_ref, sems.at[0])
    for kx in range(4):
        chi_real = bubble_ref[kx, 0]
        chi_imag = bubble_ref[kx, 1]
        spin_real, spin_imag = inverse_square(1.0 - chi_real, -chi_imag)
        charge_real, charge_imag = inverse_square(1.0 + chi_real, chi_imag)
        lanes = slice(kx * 128, kx * 128 + 128)
        weight_ref[0, :, lanes] = 1.5 * spin_real + 0.5 * charge_real - 1.0
        weight_ref[1, :, lanes] = 1.5 * spin_imag + 0.5 * charge_imag
    gone = fetch(weight_ref, weight_hbm, sems.at[1])
    table_here()
    gone()


def middle_kernel(
    in_table_ref, out_table_hbm, weight_hbm, in_ref, out_hbm,
    out_table_ref, weight_ref, out_ref, sems,
):
    left = []
    weight_here = fetch(weight_hbm, weight_ref, sems.at[1])
    out_table_here = fetch(out_table_hbm, out_table_ref, sems.at[2])
    for core in range(2):
        high, low = halves(load_columns(core, in_ref))
        chi = dot3(in_table_ref[0], in_table_ref[1], high, low)
        real, imag = chi[:128], chi[128:]
        if core == 0:
            weight_here()
        weight_real, weight_imag = weight_ref[0], weight_ref[1]
        pot = jnp.concatenate(
            [
                weight_real * real - weight_imag * imag,
                weight_real * imag + weight_imag * real,
            ],
            axis=0,
        )
        high, low = halves(pot)
        if core == 0:
            out_table_here()
        result = dot3(out_table_ref[0], out_table_ref[1], high, low)
        store_columns(result, core, out_ref)
        left.append(leave(core, out_ref, out_hbm, sems))
    for gone in left:
        gone()


def last_kernel(table_ref, in_ref, out_hbm, out_ref, sems):
    sent = []
    for core in range(2):
        high, low = halves(load_columns(core, in_ref))
        result = dot3(table_ref[0], table_ref[1], high, low)
        for kx in range(4):
            for part in range(2):
                out_ref[core, kx, part] = result[
                    part * 128 : part * 128 + 128, kx * 128 : kx * 128 + 128
                ]
        sent.append(fetch(out_ref.at[core], out_hbm.at[:, core], sems.at[core]))
    for gone in sent:
        gone()


def place_of(place):
    freq = lax.axis_index("freq")
    shift, swapped = place % 4, place // 4
    return shift // 2, lax.bitwise_xor(freq, 2 * (shift % 2) + swapped)


def gather_slab(in_ref, slot):
    return jnp.concatenate(
        [in_ref[:, freq, slot].reshape(256, 128) for freq in range(4)], axis=1
    )


def turned(real, imag, quarter):
    return ((real, imag), (-imag, real), (-real, -imag), (imag, -real))[quarter % 4]


def to_left(result, rows, left_ref):
    for high in range(4):
        lanes = slice(high * 128, high * 128 + 128)
        left_ref[high, rows, :] = jnp.concatenate(
            [result[:128, lanes], result[128:, lanes]], axis=1
        )


def to_times(step, left_ref, t_in_ref, sign):
    real, imag = left_ref[0, :, :128], left_ref[0, :, 128:]
    for high in range(1, 4):
        more = turned(left_ref[high, :, :128], left_ref[high, :, 128:], sign * high * step)
        real, imag = real + more[0], imag + more[1]
    first, second = halves(jnp.concatenate([real, imag], axis=1))
    return dot3(first, second, t_in_ref[step, 0], t_in_ref[step, 1])


def finish(x_out_ref, acc_ref, out_ref, out_hbm=None, sems=None):
    left = []
    for slab in range(2):
        rows = slice(slab * 128, slab * 128 + 128)
        source = jnp.concatenate(
            [
                jnp.concatenate([acc_ref[high, rows, :128] for high in range(4)], axis=1),
                jnp.concatenate([acc_ref[high, rows, 128:] for high in range(4)], axis=1),
            ],
            axis=0,
        )
        high, low = halves(source)
        result = dot3(x_out_ref[0], x_out_ref[1], high, low)
        for freq in range(4):
            out_ref[:, freq, slab] = result[:, freq * 128 : freq * 128 + 128].reshape(32, 8, 128)
        if out_hbm is not None:
            left.append(fetch(out_ref.at[:, :, slab], out_hbm.at[:, :, slab], sems.at[slab]))
    for gone in left:
        gone()


def accumulate(step, first, second, t_out_ref, acc_ref):
    update = dot3(first, second, t_out_ref[step, 0], t_out_ref[step, 1])
    real, imag = update[:, :128], update[:, 128:]
    for high in range(4):
        if step:
            acc_ref[high] += jnp.concatenate(turned(real, imag, high * step), axis=1)
        else:
            acc_ref[high] = update


def prepare_kernel(order_hbm, *refs):
    table_hbm, pieces, (out_hbm, table_ref, order_ref, out_ref, sems) = refs[0], refs[1:9], refs[9:]
    order_here = fetch(order_hbm, order_ref, sems.at[0])
    table_here = fetch(table_hbm, table_ref, sems.at[2])
    for place, ref in enumerate(pieces):
        arrays = ref.shape[0]
        value = jnp.concatenate(
            [
                jnp.concatenate(
                    [ref[array, pl.ds(part * 4 + block, 32, stride=8), :] for block in range(4)], axis=1
                )
                for array in range(arrays)
                for part in range(2)
            ],
            axis=0,
        )
        first = value.astype(BF16)
        rest = value - first.astype(F32)
        second, third = halves(rest)
        if place == 0:
            order_here()
        order = order_ref[...]
        moved = (dot(first, order) + dot(second, order)) + dot(third, order)
        slab, block = place_of(place)
        rows = pl.ds(pl.multiple_of(slab * 128 + block * 32, 32), 32)
        for array in range(arrays):
            for part in range(2):
                top = (array * 2 + part) * 32
                out_ref[array, part, rows, :] = moved[top : top + 32]
    gone = fetch(out_ref, out_hbm, sems.at[1])
    table_here()
    gone()


def time_lanes(step, width):
    return pl.ds(step * width, width)


def fetch_fields(field_hbm, field_ref, sems):
    return [
        fetch(
            field_hbm.at[pl.ds(0, field_ref.shape[0]), :, :, time_lanes(step, 128)],
            field_ref.at[:, :, :, time_lanes(step, 128)],
            sems.at[step],
        )
        for step in range(4)
    ]


def fetch_tables(hbm_refs, refs, sems):
    return [fetch(hbm, ref, sems.at[place]) for place, (hbm, ref) in enumerate(zip(hbm_refs, refs))]


def chi_kernel(*refs):
    x_in_ref, *tables_hbm = refs[:4]
    (in_ref, base_hbm, out_hbm, plus_hbm), tables = refs[4:8], refs[8:11]
    base_ref, plus_ref, out_ref, left_ref, acc_ref, sems, base_sems, plus_sems, out_sems = refs[11:]
    t_in_ref, t_out_ref, x_out_ref = tables
    t_in_here = fetch(tables_hbm[0], t_in_ref, sems.at[0])
    base_here = fetch_fields(base_hbm, base_ref, base_sems)
    t_out_here = fetch(tables_hbm[1], t_out_ref, sems.at[1])
    x_out_here = fetch(tables_hbm[2], x_out_ref, sems.at[2])
    site, freq = lax.axis_index("site"), lax.axis_index("freq")
    alone = jnp.logical_and(site == 0, freq < 2)
    flip = (1 - 2 * lax.rem(lax.broadcasted_iota(jnp.int32, (256, 512), 0), 2)).astype(F32).astype(BF16)

    for slab in range(2):
        high, low = halves(gather_slab(in_ref, slab))
        result = dot3(x_in_ref[0], x_in_ref[1], high, low)
        to_left(result, pl.ds(slab * 128, 128), left_ref)
        result = dot3(x_in_ref[0], x_in_ref[1], high * flip, low * flip)
        image = jnp.where(alone, slab, 1 - slab)
        rows = pl.ds(pl.multiple_of(256 + image * 128, 128), 128)
        to_left(result, rows, left_ref)

    t_in_here()
    plus_gone = []
    for step in range(4):
        times = to_times(step, left_ref, t_in_ref, -1)
        plus, minus = times[:256], times[256:]
        lanes = time_lanes(step, 256)
        plus_ref[:, lanes] = plus
        plus_gone.append(fetch(plus_ref.at[:, lanes], plus_hbm.at[:, lanes], plus_sems.at[step]))
        plus_real, plus_imag = plus[:, :128], plus[:, 128:]
        minus_real, minus_imag = minus[:, :128], -minus[:, 128:]
        base_here[step]()
        block = time_lanes(step, 128)
        base_real, base_imag = base_ref[0, 0, :, block], base_ref[0, 1, :, block]
        mirror_real, mirror_imag = base_ref[1, 0, :, block], base_ref[1, 1, :, block]
        chi_real = (
            plus_real * mirror_real - plus_imag * mirror_imag
            + base_real * minus_real - base_imag * minus_imag
        )
        chi_imag = (
            plus_real * mirror_imag + plus_imag * mirror_real
            + base_real * minus_imag + base_imag * minus_real
        )
        first, second = halves(-jnp.concatenate([chi_real, chi_imag], axis=1))
        if step == 0:
            t_out_here()
        accumulate(step, first, second, t_out_ref, acc_ref)
    x_out_here()
    finish(x_out_ref, acc_ref, out_ref, out_hbm, out_sems)
    for gone in plus_gone:
        gone()


def sigma_kernel(*refs):
    x_in_ref, *tables_hbm = refs[:4]
    in_ref, base_hbm, pot_hbm, plus_hbm, table_hbm, out_ref, table_ref = refs[4:11]
    tables, refs = refs[11:14], refs[14:]
    base_ref, pot_ref, plus_ref, left_ref, acc_ref, sems, base_sems, pot_sems, plus_sem = refs
    t_in_ref, t_out_ref, x_out_ref = tables
    t_in_here = fetch(tables_hbm[0], t_in_ref, sems.at[0])
    plus_here = fetch(plus_hbm, plus_ref, plus_sem.at[0])
    base_here = fetch_fields(base_hbm, base_ref, base_sems)
    pot_here = fetch_fields(pot_hbm, pot_ref, pot_sems)
    t_out_here = fetch(tables_hbm[1], t_out_ref, sems.at[1])
    x_out_here = fetch(tables_hbm[2], x_out_ref, sems.at[2])
    table_here = fetch(table_hbm, table_ref, plus_sem.at[1])

    for slab in range(2):
        high, low = halves(gather_slab(in_ref, slab))
        result = dot3(x_in_ref[0], x_in_ref[1], high, low)
        to_left(result, pl.ds(slab * 128, 128), left_ref)

    t_in_here()
    for step in range(4):
        change = to_times(step, left_ref, t_in_ref, -1)
        if step == 0:
            plus_here()
        base_here[step]()
        pot_here[step]()
        plus = plus_ref[:, time_lanes(step, 256)]
        block = time_lanes(step, 128)
        change_real, change_imag = change[:, :128], change[:, 128:]
        plus_real, plus_imag = plus[:, :128], plus[:, 128:]
        base_real, base_imag = base_ref[0, 0, :, block], base_ref[0, 1, :, block]
        pot_real, pot_imag = pot_ref[0, 0, :, block], pot_ref[0, 1, :, block]
        real = (
            pot_real * plus_real - pot_imag * plus_imag
            + change_real * base_real - change_imag * base_imag
        )
        imag = (
            pot_real * plus_imag + pot_imag * plus_real
            + change_real * base_imag + change_imag * base_real
        )
        first, second = halves(jnp.concatenate([real, imag], axis=1))
        if step == 0:
            t_out_here()
        accumulate(step, first, second, t_out_ref, acc_ref)
    x_out_here()
    finish(x_out_ref, acc_ref, out_ref)
    table_here()


PARAMS = pltpu.CompilerParams(vmem_limit_bytes=24 * 1024 * 1024)
WORK = 3 << 31
HBM = pl.BlockSpec(memory_space=pltpu.HBM)
HERE = pl.BlockSpec(memory_space=pltpu.VMEM)
TABLE = pl.BlockSpec(memory_space=pltpu.VMEM)


def call(body, name, in_specs, out_specs, out_shape, scratch, flops, *operands):
    size = sum(operand.size * operand.dtype.itemsize for operand in operands)
    return pl.pallas_call(
        body,
        in_specs=in_specs,
        out_specs=out_specs,
        out_shape=[
            pltpu.HBM(shape, F32) if spec is HBM else jax.ShapeDtypeStruct(shape, BF16 if spec is TABLE else F32)
            for shape, spec in zip(out_shape, out_specs)
        ],
        scratch_shapes=scratch,
        compiler_params=PARAMS,
        cost_estimate=pl.CostEstimate(flops=flops, bytes_accessed=size, transcendentals=0),
        name=name,
    )(*[
        pltpu.with_memory_space_constraint(operand, pltpu.HBM) if spec is HBM else operand
        for operand, spec in zip(operands, in_specs)
    ])


def like(array):
    return pltpu.VMEM(array.shape, array.dtype)


def sems(number):
    return pltpu.SemaphoreType.DMA((number,))


SLABS = (32, 4, 2, 8, 128)
TURN = 2 * 3 * 256 * 256 * 1024


def weight_call(bubble, table):
    shape = (2, 128, NF)
    scratch = [pltpu.VMEM(shape, F32), sems(2)]
    return call(
        weight_kernel, "weight", [HERE, HBM], [HBM, TABLE], [shape, table.shape], scratch, TURN, bubble, table
    )


def middle_call(weight, momenta, columns, held):
    scratch = [like(columns), like(weight), pltpu.VMEM((2048, 128), F32), sems(5)]
    return call(
        middle_kernel, "middle", [HERE, HBM, HBM, HERE], [HBM], [(CHIPS, 32, 128)], scratch, 2 * TURN,
        momenta, columns, weight, held,
    )[0]


def last_call(table, held):
    shape = (4, 2, 2, 128, 128)
    scratch = [pltpu.VMEM((2, 4, 2, 128, 128), F32), sems(2)]
    return call(last_kernel, "last", [HERE, HERE], [HBM], [shape], scratch, TURN, table, held)[0]


def prepare_call(pieces, table):
    shape = (pieces[0].shape[0], 2, 256, NF)
    order = jnp.asarray(t_order())
    scratch = [like(order), pltpu.VMEM(shape, F32), sems(3)]
    return call(
        prepare_kernel, "prepare", [HBM, HBM] + [HERE] * 8, [HBM, TABLE], [shape, table.shape], scratch,
        WORK, order, table, *pieces,
    )


def field(arrays):
    return pltpu.VMEM((arrays, 2, 256, NF), F32)


PLUS = (256, 1024)


def chi_call(tables, held, base):
    scratch = [
        *map(like, tables[1:]), field(2), pltpu.VMEM(PLUS, F32), pltpu.VMEM(SLABS, F32),
        pltpu.VMEM((4, 512, 256), F32), pltpu.VMEM((4, 256, 256), F32), sems(4), sems(4), sems(4), sems(2),
    ]
    return call(
        chi_kernel, "chi", [HERE, HBM, HBM, HBM, HERE, HBM], [HBM, HBM], [SLABS, PLUS], scratch, 7 * TURN,
        *tables, held.reshape(SLABS), base,
    )


def sigma_call(tables, held, base, pot, plus, table):
    scratch = [
        *map(like, tables[1:]), field(1), field(1), pltpu.VMEM(PLUS, F32),
        pltpu.VMEM((4, 256, 256), F32), pltpu.VMEM((4, 256, 256), F32), sems(4), sems(4), sems(4), sems(2),
    ]
    return call(
        sigma_kernel, "sigma", [HERE, HBM, HBM, HBM, HERE, HBM, HBM, HBM, HBM], [HERE, TABLE],
        [SLABS, table.shape], scratch, 4 * TURN, *tables, held.reshape(SLABS), base, pot, plus, table,
    )


def exchange(source):
    source = source.reshape(128, 16, 128)
    return lax.all_to_all(source, BOTH, split_axis=0, concat_axis=0, tiled=True)


def views(arrays):
    return [
        array.reshape(32, 2, 4, 4, 128).transpose(0, 1, 3, 2, 4).reshape(64, 4, 4, 1, 128)
        for array in arrays
    ]


def pieces_of(packed):
    return [piece.reshape(-1, 256, 128) for piece in packed]


def pack(array):
    shape = (1, 64, 4, 1, 128)
    return pieces_of(
        call(pack_kernel, "pack", [HBM], [HERE] * 4, [shape] * 4, [sems(4)], 1 << 20, *views([array]))
    )


def begin(arrays, table, green):
    shape = (2, 64, 4, 1, 128)
    scratch = [
        like(table), pltpu.VMEM((2, 4, 2, 128, 128), F32), pltpu.VMEM((2048, 128), F32), sems(8), sems(5)
    ]
    *packed, sent = call(
        begin_kernel, "begin", [HBM] * 4, [HERE] * 4 + [HBM], [shape] * 4 + [(CHIPS, 32, 128)],
        scratch, TURN, *views(arrays), table, green,
    )
    return pieces_of(packed), sent


def send(rows):
    return [rows[0]] + [lax.ppermute(rows[shift], BOTH, routes(shift)) for shift in (1, 2, 3)]


def both_cores(own):
    return own + [lax.ppermute(piece, "freq", [(f, f ^ 1) for f in range(4)]) for piece in own]


def local(green_tangent, green_plus, green_mirror, potential, bubble):
    columns, momenta = jnp.asarray(y_to_columns()), jnp.asarray(y_to_momenta())
    x_table, back = jnp.asarray(split(x_in(1))), jnp.asarray(x_out())
    packed, sent = begin([green_plus, green_mirror], columns, green_tangent)
    base, x_here = prepare_call(both_cores(send(packed)), x_table)
    potential, sent = lax.optimization_barrier((potential, sent))
    held = exchange(sent)
    tables = (x_here, jnp.asarray(t_in(FERMI, -1)), jnp.asarray(t_out(BOSE, 1)), back)
    sent, plus = chi_call(tables, held, base)
    potential, bubble, sent = lax.optimization_barrier((potential, bubble, sent))
    own = send(pack(potential))
    weight, momenta_here = weight_call(bubble, momenta)
    held = exchange(sent).reshape(2048, 128)
    sent = middle_call(weight, momenta_here, columns, held)
    own, sent = lax.optimization_barrier((own, sent))
    pot, x_here = prepare_call(both_cores(own), x_table)
    held = exchange(sent)
    tables = (x_here, jnp.asarray(t_in(BOSE, -1)), jnp.asarray(t_out(FERMI, 1)), back)
    sent, momenta_here = sigma_call(tables, held, base, pot, plus, momenta)
    held = exchange(sent).reshape(2048, 128)
    return last_call(momenta_here, held)


def solution(mesh):
    in_specs = (
        P("site", None, None, None, "freq"),
        P("freq", None, "site", None),
        P("freq", None, "site", None),
        P("freq", None, "site", None),
        P("site", None, None, "freq"),
    )
    out_specs = P("site", None, None, None, "freq")
    return jax.shard_map(local, mesh=mesh, in_specs=in_specs, out_specs=out_specs, check_vma=False)
```

```python
import math

import jax
import jax.numpy as jnp
import ml_dtypes
import numpy as np
from jax import lax
from jax.experimental import pallas as pl
from jax.experimental.pallas import tpu as pltpu
from jax.sharding import PartitionSpec as P

N = 128
NF = 512
BOTH = ("site", "freq")
CHIPS = 64
BF16 = jnp.bfloat16
F32 = jnp.float32


def column(chip, slab):
    site, z_hi = divmod(chip, 2)
    own = 4 * site + (z_hi if site < 16 else 2 - z_hi)
    if slab == 0:
        return own
    return (N - own) % N if own else N // 2


COLUMN = np.array([[column(chip, slab) for chip in range(CHIPS)] for slab in range(2)])


def routes(shift):
    pairs = []
    for chip in range(CHIPS):
        source = int(COLUMN[shift // 2, chip]) // 4 * 2 + (chip % 2 ^ shift % 2)
        pairs += [(2 * source + core, 2 * chip + core) for core in range(2)]
    return pairs


def phases(rows, cols, period, sign, number):
    turns = np.mod(np.outer(rows, cols), period)
    return np.exp(sign * 2j * math.pi / period * turns) / math.sqrt(number)


def real_form(matrix):
    return np.stack(
        [np.stack([matrix.real, -matrix.imag], 1), np.stack([matrix.imag, matrix.real], 1)]
    )


def split(table):
    table = table.astype(np.float32)
    high = table.astype(ml_dtypes.bfloat16)
    low = (table - high.astype(np.float32)).astype(ml_dtypes.bfloat16)
    return np.stack([high, low])


IDX = np.arange(N)
FERMI = (1 - NF) / 2
BOSE = -(NF // 2)


def y_to_columns():
    return split(real_form(phases(COLUMN.reshape(-1), IDX, N, 1, N)).reshape(256, 256))


def y_to_momenta():
    return split(real_form(phases(IDX, COLUMN.reshape(-1), N, -1, N)).reshape(256, 256))


def x_in(sign):
    return real_form(phases(IDX, IDX, N, sign, N)).transpose(0, 1, 3, 2).reshape(256, 256)


def x_out():
    return split(real_form(phases(IDX, IDX, N, -1, N)).transpose(1, 0, 2, 3).reshape(256, 256))


def t_phases(offset, sign, step):
    times = 4 * IDX + step
    return phases((IDX + offset), times, NF, sign, NF)


def t_in(offset, sign):
    tables = [real_form(t_phases(offset, sign, c).T).reshape(256, 256).T for c in range(4)]
    return split(np.stack(tables)).transpose(1, 0, 2, 3)


def t_out(offset, sign):
    tables = [real_form(t_phases(offset, sign, c)).reshape(256, 256).T for c in range(4)]
    return split(np.stack(tables)).transpose(1, 0, 2, 3)


def t_order():
    order = np.zeros((NF, NF), np.float32)
    place = np.arange(NF)
    order[4 * (place % N) + place // N, place] = 1
    return order.astype(ml_dtypes.bfloat16)


def dot(a, b):
    return lax.dot_general(a, b, (((1,), (0,)), ((), ())), preferred_element_type=F32)


def halves(value):
    high = value.astype(BF16)
    return high, (value - high.astype(F32)).astype(BF16)


def dot3(a_high, a_low, b_high, b_low):
    return dot(a_high, b_high) + (dot(a_high, b_low) + dot(a_low, b_high))


def slab_rows(core, slab, row):
    return pl.ds((core * 2 + slab) * 8 + row, CHIPS, stride=32)


def store_columns(result, core, out_ref):
    for slab in range(2):
        for kx in range(4):
            for part in range(2):
                top = part * 128 + slab * CHIPS
                out_ref[slab_rows(core, slab, kx * 2 + part), :] = result[
                    top : top + CHIPS, kx * 128 : kx * 128 + 128
                ]


def load_columns(core, in_ref):
    blocks = []
    for kx in range(4):
        pieces = []
        for part in range(2):
            for slab in range(2):
                pieces.append(in_ref[slab_rows(core, slab, kx * 2 + part), :])
        blocks.append(jnp.concatenate(pieces, axis=0))
    return jnp.concatenate(blocks, axis=1)


def fetch(source, target, sem):
    copy = pltpu.make_async_copy(source, target, sem)
    copy.start()
    return copy.wait


def leave(core, out_ref, out_hbm, sems):
    share = pl.ds(core * 16, 16)
    return fetch(out_ref.reshape(CHIPS, 32, 128).at[:, share], out_hbm.at[:, share], sems.at[3 + core])


def sort_rows(sources, outs, sems):
    site, freq = lax.axis_index("site"), lax.axis_index("freq")
    z_hi = freq // 2
    low = (z_hi, 1 - z_hi, 2 + z_hi, 3 - z_hi)
    high = (2 - z_hi, 1 + z_hi, 3 * z_hi, 3 - 3 * z_hi)
    gone = []
    for shift in (1, 2, 3, 0):
        row = jnp.where(site < 16, low[shift], high[shift])
        for array, source in enumerate(sources):
            sem = sems.at[shift * len(sources) + array]
            gone.append(fetch(source.at[:, :, row], outs[shift].at[array], sem))
    return gone


def pack_kernel(source, out0, out1, out2, out3, sems):
    for wait in sort_rows((source,), (out0, out1, out2, out3), sems):
        wait()


def begin_kernel(
    plus_hbm, mirror_hbm, table_hbm, green_hbm, out0, out1, out2, out3, out_hbm,
    table_ref, green_ref, out_ref, row_sems, sems,
):
    green_here = [fetch(green_hbm.at[:, 0], green_ref.at[0], sems.at[1])]
    table_here = fetch(table_hbm, table_ref, sems.at[0])
    rows_gone = sort_rows((plus_hbm, mirror_hbm), (out0, out1, out2, out3), row_sems)
    green_here.append(fetch(green_hbm.at[:, 1], green_ref.at[1], sems.at[2]))
    left = []
    for tangent in range(2):
        green_here[tangent]()
        source = jnp.concatenate(
            [green_ref[tangent, kx].reshape(256, 128) for kx in range(4)], axis=1
        )
        high, low = halves(source)
        if tangent == 0:
            table_here()
        result = dot3(table_ref[0], table_ref[1], high, low)
        store_columns(result, tangent, out_ref)
        left.append(leave(tangent, out_ref, out_hbm, sems))
    for wait in rows_gone + left:
        wait()


def inverse_square(real_part, imag_part):
    scale = 1.0 / (real_part * real_part + imag_part * imag_part)
    inv_real = real_part * scale
    inv_imag = -imag_part * scale
    return (inv_real * inv_real - inv_imag * inv_imag, 2.0 * inv_real * inv_imag)


def weight_kernel(bubble_ref, table_hbm, weight_ref, table_ref, sems):
    table_here = fetch(table_hbm, table_ref, sems.at[0])
    for kx in range(4):
        chi_real = bubble_ref[kx, 0]
        chi_imag = bubble_ref[kx, 1]
        spin_real, spin_imag = inverse_square(1.0 - chi_real, -chi_imag)
        charge_real, charge_imag = inverse_square(1.0 + chi_real, chi_imag)
        lanes = slice(kx * 128, kx * 128 + 128)
        weight_ref[0, :, lanes] = 1.5 * spin_real + 0.5 * charge_real - 1.0
        weight_ref[1, :, lanes] = 1.5 * spin_imag + 0.5 * charge_imag
    table_here()


def middle_kernel(
    in_table_ref, out_table_hbm, weight_ref, in_ref, out_hbm, out_table_ref, out_ref, sems
):
    left = []
    out_table_here = fetch(out_table_hbm, out_table_ref, sems.at[2])
    for core in range(2):
        high, low = halves(load_columns(core, in_ref))
        chi = dot3(in_table_ref[0], in_table_ref[1], high, low)
        real, imag = chi[:128], chi[128:]
        weight_real, weight_imag = weight_ref[0], weight_ref[1]
        pot = jnp.concatenate(
            [
                weight_real * real - weight_imag * imag,
                weight_real * imag + weight_imag * real,
            ],
            axis=0,
        )
        high, low = halves(pot)
        if core == 0:
            out_table_here()
        result = dot3(out_table_ref[0], out_table_ref[1], high, low)
        store_columns(result, core, out_ref)
        left.append(leave(core, out_ref, out_hbm, sems))
    for gone in left:
        gone()


def last_kernel(table_ref, in_ref, out_hbm, out_ref, sems):
    sent = []
    for core in range(2):
        high, low = halves(load_columns(core, in_ref))
        result = dot3(table_ref[0], table_ref[1], high, low)
        for kx in range(4):
            for part in range(2):
                out_ref[core, kx, part] = result[
                    part * 128 : part * 128 + 128, kx * 128 : kx * 128 + 128
                ]
        sent.append(fetch(out_ref.at[core], out_hbm.at[:, core], sems.at[core]))
    for gone in sent:
        gone()


def place_of(place):
    freq = lax.axis_index("freq")
    shift, swapped = place % 4, place // 4
    return shift // 2, lax.bitwise_xor(freq, 2 * (shift % 2) + swapped)


def gather_slab(in_ref, slot):
    return jnp.concatenate(
        [in_ref[:, freq, slot].reshape(256, 128) for freq in range(4)], axis=1
    )


def turned(real, imag, quarter):
    return ((real, imag), (-imag, real), (-real, -imag), (imag, -real))[quarter % 4]


def to_left(result, rows, left_ref):
    for high in range(4):
        lanes = slice(high * 128, high * 128 + 128)
        left_ref[high, rows, :] = jnp.concatenate(
            [result[:128, lanes], result[128:, lanes]], axis=1
        )


def to_times(step, left_ref, t_in_ref, sign):
    real, imag = left_ref[0, :, :128], left_ref[0, :, 128:]
    for high in range(1, 4):
        more = turned(left_ref[high, :, :128], left_ref[high, :, 128:], sign * high * step)
        real, imag = real + more[0], imag + more[1]
    first, second = halves(jnp.concatenate([real, imag], axis=1))
    return dot3(first, second, t_in_ref[step, 0], t_in_ref[step, 1])


def finish(x_out_ref, acc_ref, out_ref, out_hbm=None, sems=None):
    left = []
    for slab in range(2):
        rows = slice(slab * 128, slab * 128 + 128)
        source = jnp.concatenate(
            [
                jnp.concatenate([acc_ref[high, rows, :128] for high in range(4)], axis=1),
                jnp.concatenate([acc_ref[high, rows, 128:] for high in range(4)], axis=1),
            ],
            axis=0,
        )
        high, low = halves(source)
        result = dot3(x_out_ref[0], x_out_ref[1], high, low)
        for freq in range(4):
            out_ref[:, freq, slab] = result[:, freq * 128 : freq * 128 + 128].reshape(32, 8, 128)
        if out_hbm is not None:
            left.append(fetch(out_ref.at[:, :, slab], out_hbm.at[:, :, slab], sems.at[slab]))
    for gone in left:
        gone()


def accumulate(step, first, second, t_out_ref, acc_ref):
    update = dot3(first, second, t_out_ref[step, 0], t_out_ref[step, 1])
    real, imag = update[:, :128], update[:, 128:]
    for high in range(4):
        if step:
            acc_ref[high] += jnp.concatenate(turned(real, imag, high * step), axis=1)
        else:
            acc_ref[high] = update


def prepare_kernel(order_hbm, *refs):
    table_hbm, pieces, (out_hbm, table_ref, order_ref, out_ref, sems) = refs[0], refs[1:9], refs[9:]
    order_here = fetch(order_hbm, order_ref, sems.at[0])
    table_here = fetch(table_hbm, table_ref, sems.at[2])
    for place, ref in enumerate(pieces):
        arrays = ref.shape[0]
        value = jnp.concatenate(
            [
                jnp.concatenate(
                    [ref[array, pl.ds(part * 4 + block, 32, stride=8), :] for block in range(4)], axis=1
                )
                for array in range(arrays)
                for part in range(2)
            ],
            axis=0,
        )
        first = value.astype(BF16)
        rest = value - first.astype(F32)
        second, third = halves(rest)
        if place == 0:
            order_here()
        order = order_ref[...]
        moved = (dot(first, order) + dot(second, order)) + dot(third, order)
        slab, block = place_of(place)
        rows = pl.ds(pl.multiple_of(slab * 128 + block * 32, 32), 32)
        for array in range(arrays):
            for part in range(2):
                top = (array * 2 + part) * 32
                out_ref[array, part, rows, :] = moved[top : top + 32]
    gone = fetch(out_ref, out_hbm, sems.at[1])
    table_here()
    gone()


def time_lanes(step, width):
    return pl.ds(step * width, width)


def chi_kernel(*refs):
    x_in_ref, *tables_hbm = refs[:4]
    (in_ref, base_hbm, out_hbm, plus_hbm), tables = refs[4:8], refs[8:11]
    base_ref, plus_ref, out_ref, left_ref, acc_ref, sems, out_sems = refs[11:]
    t_in_ref, t_out_ref, x_out_ref = tables
    t_in_here = fetch(tables_hbm[0], t_in_ref, sems.at[0])
    base_here = fetch(base_hbm, base_ref, sems.at[1])
    t_out_here = fetch(tables_hbm[1], t_out_ref, sems.at[2])
    x_out_here = fetch(tables_hbm[2], x_out_ref, sems.at[3])
    site, freq = lax.axis_index("site"), lax.axis_index("freq")
    alone = jnp.logical_and(site == 0, freq < 2)
    flip = (1 - 2 * lax.rem(lax.broadcasted_iota(jnp.int32, (256, 512), 0), 2)).astype(F32).astype(BF16)

    for slab in range(2):
        high, low = halves(gather_slab(in_ref, slab))
        result = dot3(x_in_ref[0], x_in_ref[1], high, low)
        to_left(result, pl.ds(slab * 128, 128), left_ref)
        result = dot3(x_in_ref[0], x_in_ref[1], high * flip, low * flip)
        image = jnp.where(alone, slab, 1 - slab)
        rows = pl.ds(pl.multiple_of(256 + image * 128, 128), 128)
        to_left(result, rows, left_ref)

    t_in_here()
    for step in range(4):
        times = to_times(step, left_ref, t_in_ref, -1)
        plus, minus = times[:256], times[256:]
        lanes = time_lanes(step, 256)
        plus_ref[:, lanes] = plus
        plus_real, plus_imag = plus[:, :128], plus[:, 128:]
        minus_real, minus_imag = minus[:, :128], -minus[:, 128:]
        if step == 0:
            base_here()
            t_out_here()
            x_out_here()
        block = time_lanes(step, 128)
        base_real, base_imag = base_ref[0, 0, :, block], base_ref[0, 1, :, block]
        mirror_real, mirror_imag = base_ref[1, 0, :, block], base_ref[1, 1, :, block]
        chi_real = (
            plus_real * mirror_real - plus_imag * mirror_imag
            + base_real * minus_real - base_imag * minus_imag
        )
        chi_imag = (
            plus_real * mirror_imag + plus_imag * mirror_real
            + base_real * minus_imag + base_imag * minus_real
        )
        first, second = halves(-jnp.concatenate([chi_real, chi_imag], axis=1))
        accumulate(step, first, second, t_out_ref, acc_ref)
    plus_gone = fetch(plus_ref, plus_hbm, sems.at[4])
    finish(x_out_ref, acc_ref, out_ref, out_hbm, out_sems)
    plus_gone()


def sigma_kernel(*refs):
    x_in_ref, *tables_hbm = refs[:4]
    in_ref, base_hbm, pot_hbm, plus_hbm, table_hbm, out_ref, table_ref = refs[4:11]
    tables, refs = refs[11:14], refs[14:]
    base_ref, pot_ref, plus_ref, left_ref, acc_ref, sems = refs
    t_in_ref, t_out_ref, x_out_ref = tables
    t_in_here = fetch(tables_hbm[0], t_in_ref, sems.at[2])
    fields_here = [
        fetch(plus_hbm, plus_ref, sems.at[3]),
        fetch(base_hbm.at[pl.ds(0, 1)], base_ref, sems.at[4]),
        fetch(pot_hbm, pot_ref, sems.at[5]),
        fetch(tables_hbm[1], t_out_ref, sems.at[6]),
    ]
    x_out_here = fetch(tables_hbm[2], x_out_ref, sems.at[0])
    table_here = fetch(table_hbm, table_ref, sems.at[1])

    for slab in range(2):
        high, low = halves(gather_slab(in_ref, slab))
        result = dot3(x_in_ref[0], x_in_ref[1], high, low)
        to_left(result, pl.ds(slab * 128, 128), left_ref)

    t_in_here()
    for step in range(4):
        change = to_times(step, left_ref, t_in_ref, -1)
        if step == 0:
            for field_here in fields_here:
                field_here()
            x_out_here()
        plus = plus_ref[:, time_lanes(step, 256)]
        block = time_lanes(step, 128)
        change_real, change_imag = change[:, :128], change[:, 128:]
        plus_real, plus_imag = plus[:, :128], plus[:, 128:]
        base_real, base_imag = base_ref[0, 0, :, block], base_ref[0, 1, :, block]
        pot_real, pot_imag = pot_ref[0, 0, :, block], pot_ref[0, 1, :, block]
        real = (
            pot_real * plus_real - pot_imag * plus_imag
            + change_real * base_real - change_imag * base_imag
        )
        imag = (
            pot_real * plus_imag + pot_imag * plus_real
            + change_real * base_imag + change_imag * base_real
        )
        first, second = halves(jnp.concatenate([real, imag], axis=1))
        accumulate(step, first, second, t_out_ref, acc_ref)
    finish(x_out_ref, acc_ref, out_ref)
    table_here()


PARAMS = pltpu.CompilerParams(vmem_limit_bytes=24 * 1024 * 1024)
WORK = 3 << 31
HBM = pl.BlockSpec(memory_space=pltpu.HBM)
HERE = pl.BlockSpec(memory_space=pltpu.VMEM)
TABLE = pl.BlockSpec(memory_space=pltpu.VMEM)


def call(body, name, in_specs, out_specs, out_shape, scratch, flops, *operands):
    size = sum(operand.size * operand.dtype.itemsize for operand in operands)
    return pl.pallas_call(
        body,
        in_specs=in_specs,
        out_specs=out_specs,
        out_shape=[
            pltpu.HBM(shape, F32) if spec is HBM else jax.ShapeDtypeStruct(shape, BF16 if spec is TABLE else F32)
            for shape, spec in zip(out_shape, out_specs)
        ],
        scratch_shapes=scratch,
        compiler_params=PARAMS,
        cost_estimate=pl.CostEstimate(flops=flops, bytes_accessed=size, transcendentals=0),
        name=name,
    )(*[
        pltpu.with_memory_space_constraint(operand, pltpu.HBM) if spec is HBM else operand
        for operand, spec in zip(operands, in_specs)
    ])


def like(array):
    return pltpu.VMEM(array.shape, array.dtype)


def sems(number):
    return pltpu.SemaphoreType.DMA((number,))


SLABS = (32, 4, 2, 8, 128)
TURN = 2 * 3 * 256 * 256 * 1024


def weight_call(bubble, table):
    shape = (2, 128, NF)
    return call(
        weight_kernel, "weight", [HERE, HBM], [HERE, TABLE], [shape, table.shape], [sems(1)], TURN, bubble, table
    )


def middle_call(weight, momenta, columns, held):
    scratch = [like(columns), pltpu.VMEM((2048, 128), F32), sems(5)]
    return call(
        middle_kernel, "middle", [HERE, HBM, HERE, HERE], [HBM], [(CHIPS, 32, 128)], scratch, 2 * TURN,
        momenta, columns, weight, held,
    )[0]


def last_call(table, held):
    shape = (4, 2, 2, 128, 128)
    scratch = [pltpu.VMEM((2, 4, 2, 128, 128), F32), sems(2)]
    return call(last_kernel, "last", [HERE, HERE], [HBM], [shape], scratch, TURN, table, held)[0]


def prepare_call(pieces, table):
    shape = (pieces[0].shape[0], 2, 256, NF)
    order = jnp.asarray(t_order())
    scratch = [like(order), pltpu.VMEM(shape, F32), sems(3)]
    return call(
        prepare_kernel, "prepare", [HBM, HBM] + [HERE] * 8, [HBM, TABLE], [shape, table.shape], scratch,
        WORK, order, table, *pieces,
    )


def field(arrays):
    return pltpu.VMEM((arrays, 2, 256, NF), F32)


PLUS = (256, 1024)


def chi_call(tables, held, base):
    scratch = [
        *map(like, tables[1:]), field(2), pltpu.VMEM(PLUS, F32), pltpu.VMEM(SLABS, F32),
        pltpu.VMEM((4, 512, 256), F32), pltpu.VMEM((4, 256, 256), F32), sems(5), sems(2),
    ]
    return call(
        chi_kernel, "chi", [HERE, HBM, HBM, HBM, HERE, HBM], [HBM, HBM], [SLABS, PLUS], scratch, 7 * TURN,
        *tables, held.reshape(SLABS), base,
    )


def sigma_call(tables, held, base, pot, plus, table):
    scratch = [
        *map(like, tables[1:]), field(1), field(1), pltpu.VMEM(PLUS, F32),
        pltpu.VMEM((4, 256, 256), F32), pltpu.VMEM((4, 256, 256), F32), sems(7),
    ]
    return call(
        sigma_kernel, "sigma", [HERE, HBM, HBM, HBM, HERE, HBM, HBM, HBM, HBM], [HERE, TABLE],
        [SLABS, table.shape], scratch, 4 * TURN, *tables, held.reshape(SLABS), base, pot, plus, table,
    )


def exchange(source):
    source = source.reshape(128, 16, 128)
    return lax.all_to_all(source, BOTH, split_axis=0, concat_axis=0, tiled=True)


def views(arrays):
    return [
        array.reshape(32, 2, 4, 4, 128).transpose(0, 1, 3, 2, 4).reshape(64, 4, 4, 1, 128)
        for array in arrays
    ]


def pieces_of(packed):
    return [piece.reshape(-1, 256, 128) for piece in packed]


def pack(array):
    shape = (1, 64, 4, 1, 128)
    return pieces_of(
        call(pack_kernel, "pack", [HBM], [HERE] * 4, [shape] * 4, [sems(4)], 1 << 20, *views([array]))
    )


def begin(arrays, table, green):
    shape = (2, 64, 4, 1, 128)
    scratch = [
        like(table), pltpu.VMEM((2, 4, 2, 128, 128), F32), pltpu.VMEM((2048, 128), F32), sems(8), sems(5)
    ]
    *packed, sent = call(
        begin_kernel, "begin", [HBM] * 4, [HERE] * 4 + [HBM], [shape] * 4 + [(CHIPS, 32, 128)],
        scratch, TURN, *views(arrays), table, green,
    )
    return pieces_of(packed), sent


def send(rows):
    return [rows[0]] + [lax.ppermute(rows[shift], BOTH, routes(shift)) for shift in (1, 2, 3)]


def both_cores(own):
    return own + [lax.ppermute(piece, "freq", [(f, f ^ 1) for f in range(4)]) for piece in own]


def local(green_tangent, green_plus, green_mirror, potential, bubble):
    columns, momenta = jnp.asarray(y_to_columns()), jnp.asarray(y_to_momenta())
    x_table, back = jnp.asarray(split(x_in(1))), jnp.asarray(x_out())
    packed, sent = begin([green_plus, green_mirror], columns, green_tangent)
    base, x_here = prepare_call(both_cores(send(packed)), x_table)
    potential, sent = lax.optimization_barrier((potential, sent))
    held = exchange(sent)
    tables = (x_here, jnp.asarray(t_in(FERMI, -1)), jnp.asarray(t_out(BOSE, 1)), back)
    sent, plus = chi_call(tables, held, base)
    potential, bubble, sent = lax.optimization_barrier((potential, bubble, sent))
    own = send(pack(potential))
    weight, momenta_here = weight_call(bubble, momenta)
    held = exchange(sent).reshape(2048, 128)
    sent = middle_call(weight, momenta_here, columns, held)
    own, sent = lax.optimization_barrier((own, sent))
    pot, x_here = prepare_call(both_cores(own), x_table)
    held = exchange(sent)
    tables = (x_here, jnp.asarray(t_in(BOSE, -1)), jnp.asarray(t_out(FERMI, 1)), back)
    sent, momenta_here = sigma_call(tables, held, base, pot, plus, momenta)
    held = exchange(sent).reshape(2048, 128)
    return last_call(momenta_here, held)


def solution(mesh):
    in_specs = (
        P("site", None, None, None, "freq"),
        P("freq", None, "site", None),
        P("freq", None, "site", None),
        P("freq", None, "site", None),
        P("site", None, None, "freq"),
    )
    out_specs = P("site", None, None, None, "freq")
    return jax.shard_map(local, mesh=mesh, in_specs=in_specs, out_specs=out_specs, check_vma=False)
```

```python
import functools
import math

import jax
import jax.numpy as jnp
import ml_dtypes
import numpy as np
from jax import lax
from jax.experimental import pallas as pl
from jax.experimental.pallas import tpu as pltpu
from jax.sharding import PartitionSpec as P

N = 128
NF = 512
BOTH = ("site", "freq")
CHIPS = 64
BF16 = jnp.bfloat16
F32 = jnp.float32


def column(chip, slab):
    site, z_hi = divmod(chip, 2)
    own = 4 * site + (z_hi if site < 16 else 2 - z_hi)
    if slab == 0:
        return own
    return (N - own) % N if own else N // 2


COLUMN = np.array([[column(chip, slab) for chip in range(CHIPS)] for slab in range(2)])


def routes(shift):
    pairs = []
    for chip in range(CHIPS):
        source = int(COLUMN[shift // 2, chip]) // 4 * 2 + (chip % 2 ^ shift % 2)
        pairs += [(2 * source + core, 2 * chip + core) for core in range(2)]
    return pairs


def phases(rows, cols, period, sign, number):
    turns = np.mod(np.outer(rows, cols), period)
    return np.exp(sign * 2j * math.pi / period * turns) / math.sqrt(number)


def real_form(matrix):
    return np.stack(
        [np.stack([matrix.real, -matrix.imag], 1), np.stack([matrix.imag, matrix.real], 1)]
    )


def split(table):
    table = table.astype(np.float32)
    high = table.astype(ml_dtypes.bfloat16)
    low = (table - high.astype(np.float32)).astype(ml_dtypes.bfloat16)
    return np.stack([high, low])


IDX = np.arange(N)
FERMI = (1 - NF) / 2
BOSE = -(NF // 2)


def y_to_columns():
    return split(real_form(phases(COLUMN.reshape(-1), IDX, N, 1, N)).reshape(256, 256))


def y_to_momenta():
    return split(real_form(phases(IDX, COLUMN.reshape(-1), N, -1, N)).reshape(256, 256))


def x_in(sign):
    return real_form(phases(IDX, IDX, N, sign, N)).transpose(0, 1, 3, 2).reshape(256, 256)


def x_out():
    return split(real_form(phases(IDX, IDX, N, -1, N)).transpose(1, 0, 2, 3).reshape(256, 256))


def t_phases(offset, sign, step):
    times = 4 * IDX + step
    return phases((IDX + offset), times, NF, sign, NF)


def t_in(offset, sign):
    tables = [real_form(t_phases(offset, sign, c).T).reshape(256, 256).T for c in range(4)]
    return split(np.stack(tables)).transpose(1, 0, 2, 3)


def t_out(offset, sign):
    tables = [real_form(t_phases(offset, sign, c)).reshape(256, 256).T for c in range(4)]
    return split(np.stack(tables)).transpose(1, 0, 2, 3)


def t_order():
    order = np.zeros((NF, NF), np.float32)
    place = np.arange(NF)
    order[4 * (place % N) + place // N, place] = 1
    return order.astype(ml_dtypes.bfloat16)


def dot(a, b):
    return lax.dot_general(a, b, (((1,), (0,)), ((), ())), preferred_element_type=F32)


def halves(value):
    high = value.astype(BF16)
    return high, (value - high.astype(F32)).astype(BF16)


def dot3(a_high, a_low, b_high, b_low):
    return dot(a_high, b_high) + (dot(a_high, b_low) + dot(a_low, b_high))


def slab_rows(core, slab, row):
    return pl.ds((core * 2 + slab) * 8 + row, CHIPS, stride=32)


def store_columns(result, core, out_ref):
    for slab in range(2):
        for kx in range(4):
            for part in range(2):
                top = part * 128 + slab * CHIPS
                out_ref[slab_rows(core, slab, kx * 2 + part), :] = result[
                    top : top + CHIPS, kx * 128 : kx * 128 + 128
                ]


def load_columns(core, in_ref):
    blocks = []
    for kx in range(4):
        pieces = []
        for part in range(2):
            for slab in range(2):
                pieces.append(in_ref[slab_rows(core, slab, kx * 2 + part), :])
        blocks.append(jnp.concatenate(pieces, axis=0))
    return jnp.concatenate(blocks, axis=1)


def fetch(source, target, sem):
    copy = pltpu.make_async_copy(source, target, sem)
    copy.start()
    return copy.wait


def leave(core, out_ref, out_hbm, sems):
    share = pl.ds(core * 16, 16)
    return fetch(out_ref.reshape(CHIPS, 32, 128).at[:, share], out_hbm.at[:, share], sems.at[3 + core])


def sort_rows(sources, outs, sems):
    site, freq = lax.axis_index("site"), lax.axis_index("freq")
    z_hi = freq // 2
    low = (z_hi, 1 - z_hi, 2 + z_hi, 3 - z_hi)
    high = (2 - z_hi, 1 + z_hi, 3 * z_hi, 3 - 3 * z_hi)
    gone = []
    for shift in (1, 2, 3, 0):
        row = jnp.where(site < 16, low[shift], high[shift])
        for array, source in enumerate(sources):
            sem = sems.at[shift * len(sources) + array]
            gone.append(fetch(source.at[:, :, row], outs[shift].at[array], sem))
    return gone


def pack_kernel(source, out0, out1, out2, out3, sems):
    for wait in sort_rows((source,), (out0, out1, out2, out3), sems):
        wait()


def begin_kernel(
    plus_hbm, mirror_hbm, table_hbm, green_hbm, out0, out1, out2, out3, out_hbm,
    table_ref, green_ref, out_ref, row_sems, sems,
):
    green_here = [fetch(green_hbm.at[:, 0], green_ref.at[0], sems.at[1])]
    table_here = fetch(table_hbm, table_ref, sems.at[0])
    rows_gone = sort_rows((plus_hbm, mirror_hbm), (out0, out1, out2, out3), row_sems)
    green_here.append(fetch(green_hbm.at[:, 1], green_ref.at[1], sems.at[2]))
    left = []
    for tangent in range(2):
        green_here[tangent]()
        source = jnp.concatenate(
            [green_ref[tangent, kx].reshape(256, 128) for kx in range(4)], axis=1
        )
        high, low = halves(source)
        if tangent == 0:
            table_here()
        result = dot3(table_ref[0], table_ref[1], high, low)
        store_columns(result, tangent, out_ref)
        left.append(leave(tangent, out_ref, out_hbm, sems))
    for wait in rows_gone + left:
        wait()


def inverse_square(real_part, imag_part):
    scale = 1.0 / (real_part * real_part + imag_part * imag_part)
    inv_real = real_part * scale
    inv_imag = -imag_part * scale
    return (inv_real * inv_real - inv_imag * inv_imag, 2.0 * inv_real * inv_imag)


def weight_kernel(bubble_ref, table_hbm, weight_ref, table_ref, sems):
    table_here = fetch(table_hbm, table_ref, sems.at[0])
    for kx in range(4):
        chi_real = bubble_ref[kx, 0]
        chi_imag = bubble_ref[kx, 1]
        spin_real, spin_imag = inverse_square(1.0 - chi_real, -chi_imag)
        charge_real, charge_imag = inverse_square(1.0 + chi_real, chi_imag)
        lanes = slice(kx * 128, kx * 128 + 128)
        weight_ref[0, :, lanes] = 1.5 * spin_real + 0.5 * charge_real - 1.0
        weight_ref[1, :, lanes] = 1.5 * spin_imag + 0.5 * charge_imag
    table_here()


def middle_kernel(
    in_table_ref, out_table_hbm, weight_ref, in_ref, out_hbm, out_table_ref, out_ref, sems
):
    left = []
    out_table_here = fetch(out_table_hbm, out_table_ref, sems.at[2])
    for core in range(2):
        high, low = halves(load_columns(core, in_ref))
        chi = dot3(in_table_ref[0], in_table_ref[1], high, low)
        real, imag = chi[:128], chi[128:]
        weight_real, weight_imag = weight_ref[0], weight_ref[1]
        pot = jnp.concatenate(
            [
                weight_real * real - weight_imag * imag,
                weight_real * imag + weight_imag * real,
            ],
            axis=0,
        )
        high, low = halves(pot)
        if core == 0:
            out_table_here()
        result = dot3(out_table_ref[0], out_table_ref[1], high, low)
        store_columns(result, core, out_ref)
        left.append(leave(core, out_ref, out_hbm, sems))
    for gone in left:
        gone()


def last_kernel(table_ref, in_ref, out_hbm, out_ref, sems):
    sent = []
    for core in range(2):
        high, low = halves(load_columns(core, in_ref))
        result = dot3(table_ref[0], table_ref[1], high, low)
        for kx in range(4):
            for part in range(2):
                out_ref[core, kx, part] = result[
                    part * 128 : part * 128 + 128, kx * 128 : kx * 128 + 128
                ]
        sent.append(fetch(out_ref.at[core], out_hbm.at[:, core], sems.at[core]))
    for gone in sent:
        gone()


def place_of(place):
    freq = lax.axis_index("freq")
    shift, swapped = place % 4, place // 4
    return shift // 2, lax.bitwise_xor(freq, 2 * (shift % 2) + swapped)


def gather_slab(in_ref, slot):
    return jnp.concatenate(
        [in_ref[:, freq, slot].reshape(256, 128) for freq in range(4)], axis=1
    )


def turned(real, imag, quarter):
    return ((real, imag), (-imag, real), (-real, -imag), (imag, -real))[quarter % 4]


def to_left(result, rows, left_ref):
    for high in range(4):
        lanes = slice(high * 128, high * 128 + 128)
        left_ref[high, rows, :] = jnp.concatenate(
            [result[:128, lanes], result[128:, lanes]], axis=1
        )


def to_times(step, left_ref, t_in_ref, sign):
    real, imag = left_ref[0, :, :128], left_ref[0, :, 128:]
    for high in range(1, 4):
        more = turned(left_ref[high, :, :128], left_ref[high, :, 128:], sign * high * step)
        real, imag = real + more[0], imag + more[1]
    first, second = halves(jnp.concatenate([real, imag], axis=1))
    return dot3(first, second, t_in_ref[step, 0], t_in_ref[step, 1])


def finish(x_out_ref, acc_ref, out_ref, out_hbm=None, sems=None):
    left = []
    for slab in range(2):
        rows = slice(slab * 128, slab * 128 + 128)
        source = jnp.concatenate(
            [
                jnp.concatenate([acc_ref[high, rows, :128] for high in range(4)], axis=1),
                jnp.concatenate([acc_ref[high, rows, 128:] for high in range(4)], axis=1),
            ],
            axis=0,
        )
        high, low = halves(source)
        result = dot3(x_out_ref[0], x_out_ref[1], high, low)
        for freq in range(4):
            out_ref[:, freq, slab] = result[:, freq * 128 : freq * 128 + 128].reshape(32, 8, 128)
        if out_hbm is not None:
            left.append(fetch(out_ref.at[:, :, slab], out_hbm.at[:, :, slab], sems.at[slab]))
    for gone in left:
        gone()


def accumulate(step, first, second, t_out_ref, acc_ref):
    update = dot3(first, second, t_out_ref[step, 0], t_out_ref[step, 1])
    real, imag = update[:, :128], update[:, 128:]
    for high in range(4):
        if step:
            acc_ref[high] += jnp.concatenate(turned(real, imag, high * step), axis=1)
        else:
            acc_ref[high] = update


def prepare_kernel(count, stay, order_hbm, *refs):
    tables_hbm, pieces, tables = refs[:count], refs[count : count + 8], refs[count + 8 : 2 * count + 8]
    result, order_ref, sems, *rest = refs[2 * count + 8 :]
    out_ref = result if stay else rest[0]
    order_here = fetch(order_hbm, order_ref, sems.at[0])
    tables_here = [
        fetch(hbm, ref, sems.at[2 + place]) for place, (hbm, ref) in enumerate(zip(tables_hbm, tables))
    ]
    for place, ref in enumerate(pieces):
        arrays = ref.shape[0]
        value = jnp.concatenate(
            [
                jnp.concatenate(
                    [ref[array, pl.ds(part * 4 + block, 32, stride=8), :] for block in range(4)], axis=1
                )
                for array in range(arrays)
                for part in range(2)
            ],
            axis=0,
        )
        first = value.astype(BF16)
        rest = value - first.astype(F32)
        second, third = halves(rest)
        if place == 0:
            order_here()
        order = order_ref[...]
        moved = (dot(first, order) + dot(second, order)) + dot(third, order)
        slab, block = place_of(place)
        rows = pl.ds(pl.multiple_of(slab * 128 + block * 32, 32), 32)
        for array in range(arrays):
            for part in range(2):
                top = (array * 2 + part) * 32
                out_ref[array, part, rows, :] = moved[top : top + 32]
    if not stay:
        fetch(out_ref, result, sems.at[1])()
    for table_here in tables_here:
        table_here()


def time_lanes(step, width):
    return pl.ds(step * width, width)


def chi_kernel(*refs):
    x_in_ref, *tables_hbm = refs[:4]
    (in_ref, base_hbm, out_hbm, plus_hbm), tables = refs[4:8], refs[8:11]
    base_ref, plus_ref, out_ref, left_ref, acc_ref, sems, out_sems = refs[11:]
    t_in_ref, t_out_ref, x_out_ref = tables
    t_in_here = fetch(tables_hbm[0], t_in_ref, sems.at[0])
    base_here = fetch(base_hbm, base_ref, sems.at[1])
    t_out_here = fetch(tables_hbm[1], t_out_ref, sems.at[2])
    x_out_here = fetch(tables_hbm[2], x_out_ref, sems.at[3])
    site, freq = lax.axis_index("site"), lax.axis_index("freq")
    alone = jnp.logical_and(site == 0, freq < 2)
    flip = (1 - 2 * lax.rem(lax.broadcasted_iota(jnp.int32, (256, 512), 0), 2)).astype(F32).astype(BF16)

    for slab in range(2):
        high, low = halves(gather_slab(in_ref, slab))
        result = dot3(x_in_ref[0], x_in_ref[1], high, low)
        to_left(result, pl.ds(slab * 128, 128), left_ref)
        result = dot3(x_in_ref[0], x_in_ref[1], high * flip, low * flip)
        image = jnp.where(alone, slab, 1 - slab)
        rows = pl.ds(pl.multiple_of(256 + image * 128, 128), 128)
        to_left(result, rows, left_ref)

    t_in_here()
    for step in range(4):
        times = to_times(step, left_ref, t_in_ref, -1)
        plus, minus = times[:256], times[256:]
        lanes = time_lanes(step, 256)
        plus_ref[:, lanes] = plus
        plus_real, plus_imag = plus[:, :128], plus[:, 128:]
        minus_real, minus_imag = minus[:, :128], -minus[:, 128:]
        if step == 0:
            base_here()
        block = time_lanes(step, 128)
        base_real, base_imag = base_ref[0, 0, :, block], base_ref[0, 1, :, block]
        mirror_real, mirror_imag = base_ref[1, 0, :, block], base_ref[1, 1, :, block]
        chi_real = (
            plus_real * mirror_real - plus_imag * mirror_imag
            + base_real * minus_real - base_imag * minus_imag
        )
        chi_imag = (
            plus_real * mirror_imag + plus_imag * mirror_real
            + base_real * minus_imag + base_imag * minus_real
        )
        first, second = halves(-jnp.concatenate([chi_real, chi_imag], axis=1))
        if step == 0:
            t_out_here()
        accumulate(step, first, second, t_out_ref, acc_ref)
    x_out_here()
    plus_gone = fetch(plus_ref, plus_hbm, sems.at[4])
    finish(x_out_ref, acc_ref, out_ref, out_hbm, out_sems)
    plus_gone()


def sigma_kernel(*refs):
    x_in_ref, *tables_hbm = refs[:4]
    in_ref, base_hbm, pot_ref, plus_hbm, table_hbm, out_ref, table_ref = refs[4:11]
    tables, refs = refs[11:14], refs[14:]
    base_ref, plus_ref, left_ref, acc_ref, sems = refs
    t_in_ref, t_out_ref, x_out_ref = tables
    t_in_here = fetch(tables_hbm[0], t_in_ref, sems.at[2])
    fields_here = [
        fetch(plus_hbm, plus_ref, sems.at[3]),
        fetch(base_hbm.at[pl.ds(0, 1)], base_ref, sems.at[4]),
    ]
    t_out_here = fetch(tables_hbm[1], t_out_ref, sems.at[6])
    x_out_here = fetch(tables_hbm[2], x_out_ref, sems.at[0])
    table_here = fetch(table_hbm, table_ref, sems.at[1])

    for slab in range(2):
        high, low = halves(gather_slab(in_ref, slab))
        result = dot3(x_in_ref[0], x_in_ref[1], high, low)
        to_left(result, pl.ds(slab * 128, 128), left_ref)

    t_in_here()
    for step in range(4):
        change = to_times(step, left_ref, t_in_ref, -1)
        if step == 0:
            for field_here in fields_here:
                field_here()
        plus = plus_ref[:, time_lanes(step, 256)]
        block = time_lanes(step, 128)
        change_real, change_imag = change[:, :128], change[:, 128:]
        plus_real, plus_imag = plus[:, :128], plus[:, 128:]
        base_real, base_imag = base_ref[0, 0, :, block], base_ref[0, 1, :, block]
        pot_real, pot_imag = pot_ref[0, 0, :, block], pot_ref[0, 1, :, block]
        real = (
            pot_real * plus_real - pot_imag * plus_imag
            + change_real * base_real - change_imag * base_imag
        )
        imag = (
            pot_real * plus_imag + pot_imag * plus_real
            + change_real * base_imag + change_imag * base_real
        )
        first, second = halves(jnp.concatenate([real, imag], axis=1))
        if step == 0:
            t_out_here()
        accumulate(step, first, second, t_out_ref, acc_ref)
    x_out_here()
    finish(x_out_ref, acc_ref, out_ref)
    table_here()


PARAMS = pltpu.CompilerParams(vmem_limit_bytes=24 * 1024 * 1024)
WORK = 3 << 31
HBM = pl.BlockSpec(memory_space=pltpu.HBM)
HERE = pl.BlockSpec(memory_space=pltpu.VMEM)
TABLE = pl.BlockSpec(memory_space=pltpu.VMEM)


def call(body, name, in_specs, out_specs, out_shape, scratch, flops, *operands):
    size = sum(operand.size * operand.dtype.itemsize for operand in operands)
    return pl.pallas_call(
        body,
        in_specs=in_specs,
        out_specs=out_specs,
        out_shape=[
            pltpu.HBM(shape, F32) if spec is HBM else jax.ShapeDtypeStruct(shape, BF16 if spec is TABLE else F32)
            for shape, spec in zip(out_shape, out_specs)
        ],
        scratch_shapes=scratch,
        compiler_params=PARAMS,
        cost_estimate=pl.CostEstimate(flops=flops, bytes_accessed=size, transcendentals=0),
        name=name,
    )(*[
        pltpu.with_memory_space_constraint(operand, pltpu.HBM) if spec is HBM else operand
        for operand, spec in zip(operands, in_specs)
    ])


def like(array):
    return pltpu.VMEM(array.shape, array.dtype)


def sems(number):
    return pltpu.SemaphoreType.DMA((number,))


SLABS = (32, 4, 2, 8, 128)
TURN = 2 * 3 * 256 * 256 * 1024


def weight_call(bubble, table):
    shape = (2, 128, NF)
    return call(
        weight_kernel, "weight", [HERE, HBM], [HERE, TABLE], [shape, table.shape], [sems(1)], TURN, bubble, table
    )


def middle_call(weight, momenta, columns, held):
    scratch = [like(columns), pltpu.VMEM((2048, 128), F32), sems(5)]
    return call(
        middle_kernel, "middle", [HERE, HBM, HERE, HERE], [HBM], [(CHIPS, 32, 128)], scratch, 2 * TURN,
        momenta, columns, weight, held,
    )[0]


def last_call(table, held):
    shape = (4, 2, 2, 128, 128)
    scratch = [pltpu.VMEM((2, 4, 2, 128, 128), F32), sems(2)]
    return call(last_kernel, "last", [HERE, HERE], [HBM], [shape], scratch, TURN, table, held)[0]


def prepare_call(pieces, tables, stay):
    shape = (pieces[0].shape[0], 2, 256, NF)
    order = jnp.asarray(t_order())
    count = len(tables)
    return call(
        functools.partial(prepare_kernel, count, stay), "prepare", [HBM] * (1 + count) + [HERE] * 8,
        [TABLE] * count + [HERE if stay else HBM], [*(table.shape for table in tables), shape],
        [like(order), sems(2 + count)] + ([] if stay else [pltpu.VMEM(shape, F32)]),
        WORK, order, *tables, *pieces,
    )


def field(arrays):
    return pltpu.VMEM((arrays, 2, 256, NF), F32)


PLUS = (256, 1024)


def chi_call(tables, held, base):
    scratch = [
        *map(like, tables[1:]), field(2), pltpu.VMEM(PLUS, F32), pltpu.VMEM(SLABS, F32),
        pltpu.VMEM((4, 512, 256), F32), pltpu.VMEM((4, 256, 256), F32), sems(5), sems(2),
    ]
    return call(
        chi_kernel, "chi", [HERE, HBM, HBM, HBM, HERE, HBM], [HBM, HBM], [SLABS, PLUS], scratch, 7 * TURN,
        *tables, held.reshape(SLABS), base,
    )


def sigma_call(tables, held, base, pot, plus, table):
    scratch = [
        *map(like, tables[1:]), field(1), pltpu.VMEM(PLUS, F32),
        pltpu.VMEM((4, 256, 256), F32), pltpu.VMEM((4, 256, 256), F32), sems(7),
    ]
    return call(
        sigma_kernel, "sigma", [HERE, HBM, HBM, HBM, HERE, HBM, HERE, HBM, HBM], [HERE, TABLE],
        [SLABS, table.shape], scratch, 4 * TURN, *tables, held.reshape(SLABS), base, pot, plus, table,
    )


def exchange(source):
    source = source.reshape(128, 16, 128)
    return lax.all_to_all(source, BOTH, split_axis=0, concat_axis=0, tiled=True)


def views(arrays):
    return [
        array.reshape(32, 2, 4, 4, 128).transpose(0, 1, 3, 2, 4).reshape(64, 4, 4, 1, 128)
        for array in arrays
    ]


def pieces_of(packed):
    return [piece.reshape(-1, 256, 128) for piece in packed]


def pack(array):
    shape = (1, 64, 4, 1, 128)
    return pieces_of(
        call(pack_kernel, "pack", [HBM], [HERE] * 4, [shape] * 4, [sems(4)], 1 << 20, *views([array]))
    )


def begin(arrays, table, green):
    shape = (2, 64, 4, 1, 128)
    scratch = [
        like(table), pltpu.VMEM((2, 4, 2, 128, 128), F32), pltpu.VMEM((2048, 128), F32), sems(8), sems(5)
    ]
    *packed, sent = call(
        begin_kernel, "begin", [HBM] * 4, [HERE] * 4 + [HBM], [shape] * 4 + [(CHIPS, 32, 128)],
        scratch, TURN, *views(arrays), table, green,
    )
    return pieces_of(packed), sent


def send(rows):
    return [rows[0]] + [lax.ppermute(rows[shift], BOTH, routes(shift)) for shift in (1, 2, 3)]


def both_cores(own):
    return own + [lax.ppermute(piece, "freq", [(f, f ^ 1) for f in range(4)]) for piece in own]


def local(green_tangent, green_plus, green_mirror, potential, bubble):
    columns, momenta = jnp.asarray(y_to_columns()), jnp.asarray(y_to_momenta())
    x_table, back = jnp.asarray(split(x_in(1))), jnp.asarray(x_out())
    packed, sent = begin([green_plus, green_mirror], columns, green_tangent)
    x_here, base = prepare_call(both_cores(send(packed)), [x_table], False)
    potential, sent = lax.optimization_barrier((potential, sent))
    held = exchange(sent)
    tables = (x_here, jnp.asarray(t_in(FERMI, -1)), jnp.asarray(t_out(BOSE, 1)), back)
    sent, plus = chi_call(tables, held, base)
    potential, bubble, sent = lax.optimization_barrier((potential, bubble, sent))
    own = send(pack(potential))
    weight, momenta_here = weight_call(bubble, momenta)
    held = exchange(sent).reshape(2048, 128)
    sent = middle_call(weight, momenta_here, columns, held)
    own, sent = lax.optimization_barrier((own, sent))
    x_here, pot = prepare_call(both_cores(own), [x_table], True)
    held = exchange(sent)
    tables = (x_here, jnp.asarray(t_in(BOSE, -1)), jnp.asarray(t_out(FERMI, 1)), back)
    sent, momenta_here = sigma_call(tables, held, base, pot, plus, momenta)
    held = exchange(sent).reshape(2048, 128)
    return last_call(momenta_here, held)


def solution(mesh):
    in_specs = (
        P("site", None, None, None, "freq"),
        P("freq", None, "site", None),
        P("freq", None, "site", None),
        P("freq", None, "site", None),
        P("site", None, None, "freq"),
    )
    out_specs = P("site", None, None, None, "freq")
    return jax.shard_map(local, mesh=mesh, in_specs=in_specs, out_specs=out_specs, check_vma=False)
```

```python
import functools
import math

import jax
import jax.numpy as jnp
import ml_dtypes
import numpy as np
from jax import lax
from jax.experimental import pallas as pl
from jax.experimental.pallas import tpu as pltpu
from jax.sharding import PartitionSpec as P

N = 128
NF = 512
BOTH = ("site", "freq")
CHIPS = 64
BF16 = jnp.bfloat16
F32 = jnp.float32


def column(chip, slab):
    site, z_hi = divmod(chip, 2)
    own = 4 * site + (z_hi if site < 16 else 2 - z_hi)
    if slab == 0:
        return own
    return (N - own) % N if own else N // 2


COLUMN = np.array([[column(chip, slab) for chip in range(CHIPS)] for slab in range(2)])


def routes(shift):
    pairs = []
    for chip in range(CHIPS):
        source = int(COLUMN[shift // 2, chip]) // 4 * 2 + (chip % 2 ^ shift % 2)
        pairs += [(2 * source + core, 2 * chip + core) for core in range(2)]
    return pairs


def phases(rows, cols, period, sign, number):
    turns = np.mod(np.outer(rows, cols), period)
    return np.exp(sign * 2j * math.pi / period * turns) / math.sqrt(number)


def real_form(matrix):
    return np.stack(
        [np.stack([matrix.real, -matrix.imag], 1), np.stack([matrix.imag, matrix.real], 1)]
    )


def split(table):
    table = table.astype(np.float32)
    high = table.astype(ml_dtypes.bfloat16)
    low = (table - high.astype(np.float32)).astype(ml_dtypes.bfloat16)
    return np.stack([high, low])


IDX = np.arange(N)
FERMI = (1 - NF) / 2
BOSE = -(NF // 2)


def y_to_columns():
    return split(real_form(phases(COLUMN.reshape(-1), IDX, N, 1, N)).reshape(256, 256))


def y_to_momenta():
    return split(real_form(phases(IDX, COLUMN.reshape(-1), N, -1, N)).reshape(256, 256))


def x_in(sign):
    return real_form(phases(IDX, IDX, N, sign, N)).transpose(0, 1, 3, 2).reshape(256, 256)


def x_out():
    return split(real_form(phases(IDX, IDX, N, -1, N)).transpose(1, 0, 2, 3).reshape(256, 256))


def t_phases(offset, sign, step):
    times = 4 * IDX + step
    return phases((IDX + offset), times, NF, sign, NF)


def t_in(offset, sign):
    tables = [real_form(t_phases(offset, sign, c).T).reshape(256, 256).T for c in range(4)]
    return split(np.stack(tables)).transpose(1, 0, 2, 3)


def t_out(offset, sign):
    tables = [real_form(t_phases(offset, sign, c)).reshape(256, 256).T for c in range(4)]
    return split(np.stack(tables)).transpose(1, 0, 2, 3)


def t_order():
    order = np.zeros((NF, NF), np.float32)
    place = np.arange(NF)
    order[4 * (place % N) + place // N, place] = 1
    return order.astype(ml_dtypes.bfloat16)


def dot(a, b):
    return lax.dot_general(a, b, (((1,), (0,)), ((), ())), preferred_element_type=F32)


def halves(value):
    high = value.astype(BF16)
    return high, (value - high.astype(F32)).astype(BF16)


def dot3(a_high, a_low, b_high, b_low):
    return dot(a_high, b_high) + (dot(a_high, b_low) + dot(a_low, b_high))


def slab_rows(core, slab, row):
    return pl.ds((core * 2 + slab) * 8 + row, CHIPS, stride=32)


def store_columns(result, core, out_ref):
    for slab in range(2):
        for kx in range(4):
            for part in range(2):
                top = part * 128 + slab * CHIPS
                out_ref[slab_rows(core, slab, kx * 2 + part), :] = result[
                    top : top + CHIPS, kx * 128 : kx * 128 + 128
                ]


def load_columns(core, in_ref):
    blocks = []
    for kx in range(4):
        pieces = []
        for part in range(2):
            for slab in range(2):
                pieces.append(in_ref[slab_rows(core, slab, kx * 2 + part), :])
        blocks.append(jnp.concatenate(pieces, axis=0))
    return jnp.concatenate(blocks, axis=1)


def fetch(source, target, sem):
    copy = pltpu.make_async_copy(source, target, sem)
    copy.start()
    return copy.wait


def leave(core, out_ref, out_hbm, sems):
    share = pl.ds(core * 16, 16)
    return fetch(out_ref.reshape(CHIPS, 32, 128).at[:, share], out_hbm.at[:, share], sems.at[3 + core])


def sort_rows(sources, outs, sems):
    site, freq = lax.axis_index("site"), lax.axis_index("freq")
    z_hi = freq // 2
    low = (z_hi, 1 - z_hi, 2 + z_hi, 3 - z_hi)
    high = (2 - z_hi, 1 + z_hi, 3 * z_hi, 3 - 3 * z_hi)
    gone = []
    for shift in (1, 2, 3, 0):
        row = jnp.where(site < 16, low[shift], high[shift])
        for array, source in enumerate(sources):
            sem = sems.at[shift * len(sources) + array]
            gone.append(fetch(source.at[:, :, row], outs[shift].at[array], sem))
    return gone


def pack_kernel(source, out0, out1, out2, out3, sems):
    for wait in sort_rows((source,), (out0, out1, out2, out3), sems):
        wait()


def begin_kernel(
    plus_hbm, mirror_hbm, table_hbm, green_hbm, out0, out1, out2, out3, out_hbm,
    table_ref, green_ref, out_ref, row_sems, sems,
):
    green_here = [fetch(green_hbm.at[:, 0], green_ref.at[0], sems.at[1])]
    table_here = fetch(table_hbm, table_ref, sems.at[0])
    rows_gone = sort_rows((plus_hbm, mirror_hbm), (out0, out1, out2, out3), row_sems)
    green_here.append(fetch(green_hbm.at[:, 1], green_ref.at[1], sems.at[2]))
    left = []
    for tangent in range(2):
        green_here[tangent]()
        source = jnp.concatenate(
            [green_ref[tangent, kx].reshape(256, 128) for kx in range(4)], axis=1
        )
        high, low = halves(source)
        if tangent == 0:
            table_here()
        result = dot3(table_ref[0], table_ref[1], high, low)
        store_columns(result, tangent, out_ref)
        left.append(leave(tangent, out_ref, out_hbm, sems))
    for wait in rows_gone + left:
        wait()


def inverse_square(real_part, imag_part):
    scale = 1.0 / (real_part * real_part + imag_part * imag_part)
    inv_real = real_part * scale
    inv_imag = -imag_part * scale
    return (inv_real * inv_real - inv_imag * inv_imag, 2.0 * inv_real * inv_imag)


def weight_kernel(bubble_ref, table_hbm, weight_ref, table_ref, sems):
    table_here = fetch(table_hbm, table_ref, sems.at[0])
    for kx in range(4):
        chi_real = bubble_ref[kx, 0]
        chi_imag = bubble_ref[kx, 1]
        spin_real, spin_imag = inverse_square(1.0 - chi_real, -chi_imag)
        charge_real, charge_imag = inverse_square(1.0 + chi_real, chi_imag)
        lanes = slice(kx * 128, kx * 128 + 128)
        weight_ref[0, :, lanes] = 1.5 * spin_real + 0.5 * charge_real - 1.0
        weight_ref[1, :, lanes] = 1.5 * spin_imag + 0.5 * charge_imag
    table_here()


def middle_kernel(
    in_table_ref, out_table_hbm, weight_ref, in_ref, out_hbm, out_table_ref, out_ref, sems
):
    left = []
    out_table_here = fetch(out_table_hbm, out_table_ref, sems.at[2])
    for core in range(2):
        high, low = halves(load_columns(core, in_ref))
        chi = dot3(in_table_ref[0], in_table_ref[1], high, low)
        real, imag = chi[:128], chi[128:]
        weight_real, weight_imag = weight_ref[0], weight_ref[1]
        pot = jnp.concatenate(
            [
                weight_real * real - weight_imag * imag,
                weight_real * imag + weight_imag * real,
            ],
            axis=0,
        )
        high, low = halves(pot)
        if core == 0:
            out_table_here()
        result = dot3(out_table_ref[0], out_table_ref[1], high, low)
        store_columns(result, core, out_ref)
        left.append(leave(core, out_ref, out_hbm, sems))
    for gone in left:
        gone()


def last_kernel(table_ref, in_ref, out_hbm, out_ref, sems):
    sent = []
    for core in range(2):
        high, low = halves(load_columns(core, in_ref))
        result = dot3(table_ref[0], table_ref[1], high, low)
        for kx in range(4):
            for part in range(2):
                out_ref[core, kx, part] = result[
                    part * 128 : part * 128 + 128, kx * 128 : kx * 128 + 128
                ]
        sent.append(fetch(out_ref.at[core], out_hbm.at[:, core], sems.at[core]))
    for gone in sent:
        gone()


def place_of(place):
    freq = lax.axis_index("freq")
    shift, swapped = place % 4, place // 4
    return shift // 2, lax.bitwise_xor(freq, 2 * (shift % 2) + swapped)


def gather_slab(in_ref, slot):
    return jnp.concatenate(
        [in_ref[:, freq, slot].reshape(256, 128) for freq in range(4)], axis=1
    )


def turned(real, imag, quarter):
    return ((real, imag), (-imag, real), (-real, -imag), (imag, -real))[quarter % 4]


def to_left(result, rows, left_ref):
    for high in range(4):
        lanes = slice(high * 128, high * 128 + 128)
        left_ref[high, rows, :] = jnp.concatenate(
            [result[:128, lanes], result[128:, lanes]], axis=1
        )


def to_times(step, left_ref, t_in_ref, sign):
    real, imag = left_ref[0, :, :128], left_ref[0, :, 128:]
    for high in range(1, 4):
        more = turned(left_ref[high, :, :128], left_ref[high, :, 128:], sign * high * step)
        real, imag = real + more[0], imag + more[1]
    first, second = halves(jnp.concatenate([real, imag], axis=1))
    return dot3(first, second, t_in_ref[step, 0], t_in_ref[step, 1])


def finish(x_out_ref, acc_ref, out_ref, out_hbm=None, sems=None):
    left = []
    for slab in range(2):
        rows = slice(slab * 128, slab * 128 + 128)
        source = jnp.concatenate(
            [
                jnp.concatenate([acc_ref[high, rows, :128] for high in range(4)], axis=1),
                jnp.concatenate([acc_ref[high, rows, 128:] for high in range(4)], axis=1),
            ],
            axis=0,
        )
        high, low = halves(source)
        result = dot3(x_out_ref[0], x_out_ref[1], high, low)
        for freq in range(4):
            out_ref[:, freq, slab] = result[:, freq * 128 : freq * 128 + 128].reshape(32, 8, 128)
        if out_hbm is not None:
            left.append(fetch(out_ref.at[:, :, slab], out_hbm.at[:, :, slab], sems.at[slab]))
    for gone in left:
        gone()


def accumulate(step, first, second, t_out_ref, acc_ref):
    update = dot3(first, second, t_out_ref[step, 0], t_out_ref[step, 1])
    real, imag = update[:, :128], update[:, 128:]
    for high in range(4):
        if step:
            acc_ref[high] += jnp.concatenate(turned(real, imag, high * step), axis=1)
        else:
            acc_ref[high] = update


def prepare_kernel(count, stay, order_hbm, *refs):
    tables_hbm, pieces, tables = refs[:count], refs[count : count + 8], refs[count + 8 : 2 * count + 8]
    result, order_ref, sems, *rest = refs[2 * count + 8 :]
    out_ref = result if stay else rest[0]
    order_here = fetch(order_hbm, order_ref, sems.at[0])
    tables_here = [
        fetch(hbm, ref, sems.at[2 + place]) for place, (hbm, ref) in enumerate(zip(tables_hbm, tables))
    ]
    for place, ref in enumerate(pieces):
        arrays = ref.shape[0]
        value = jnp.concatenate(
            [
                jnp.concatenate(
                    [ref[array, pl.ds(part * 4 + block, 32, stride=8), :] for block in range(4)], axis=1
                )
                for array in range(arrays)
                for part in range(2)
            ],
            axis=0,
        )
        first = value.astype(BF16)
        rest = value - first.astype(F32)
        second, third = halves(rest)
        if place == 0:
            order_here()
        order = order_ref[...]
        moved = (dot(first, order) + dot(second, order)) + dot(third, order)
        slab, block = place_of(place)
        rows = pl.ds(pl.multiple_of(slab * 128 + block * 32, 32), 32)
        for array in range(arrays):
            for part in range(2):
                top = (array * 2 + part) * 32
                out_ref[array, part, rows, :] = moved[top : top + 32]
    if not stay:
        fetch(out_ref, result, sems.at[1])()
    for table_here in tables_here:
        table_here()


def time_lanes(step, width):
    return pl.ds(step * width, width)


def chi_kernel(*refs):
    x_in_ref, *tables_hbm = refs[:4]
    (in_ref, base_hbm, out_hbm, plus_hbm), tables = refs[4:8], refs[8:11]
    base_ref, plus_ref, out_ref, left_ref, acc_ref, sems, out_sems = refs[11:]
    t_in_ref, t_out_ref, x_out_ref = tables
    t_in_here = fetch(tables_hbm[0], t_in_ref, sems.at[0])
    base_here = fetch(base_hbm, base_ref, sems.at[1])
    t_out_here = fetch(tables_hbm[1], t_out_ref, sems.at[2])
    x_out_here = fetch(tables_hbm[2], x_out_ref, sems.at[3])
    site, freq = lax.axis_index("site"), lax.axis_index("freq")
    alone = jnp.logical_and(site == 0, freq < 2)
    flip = (1 - 2 * lax.rem(lax.broadcasted_iota(jnp.int32, (256, 512), 0), 2)).astype(F32).astype(BF16)

    for slab in range(2):
        high, low = halves(gather_slab(in_ref, slab))
        result = dot3(x_in_ref[0], x_in_ref[1], high, low)
        to_left(result, pl.ds(slab * 128, 128), left_ref)
        result = dot3(x_in_ref[0], x_in_ref[1], high * flip, low * flip)
        image = jnp.where(alone, slab, 1 - slab)
        rows = pl.ds(pl.multiple_of(256 + image * 128, 128), 128)
        to_left(result, rows, left_ref)

    t_in_here()
    for step in range(4):
        times = to_times(step, left_ref, t_in_ref, -1)
        plus, minus = times[:256], times[256:]
        lanes = time_lanes(step, 256)
        plus_ref[:, lanes] = plus
        plus_real, plus_imag = plus[:, :128], plus[:, 128:]
        minus_real, minus_imag = minus[:, :128], -minus[:, 128:]
        if step == 0:
            base_here()
        block = time_lanes(step, 128)
        base_real, base_imag = base_ref[0, 0, :, block], base_ref[0, 1, :, block]
        mirror_real, mirror_imag = base_ref[1, 0, :, block], base_ref[1, 1, :, block]
        chi_real = (
            plus_real * mirror_real - plus_imag * mirror_imag
            + base_real * minus_real - base_imag * minus_imag
        )
        chi_imag = (
            plus_real * mirror_imag + plus_imag * mirror_real
            + base_real * minus_imag + base_imag * minus_real
        )
        first, second = halves(-jnp.concatenate([chi_real, chi_imag], axis=1))
        if step == 0:
            t_out_here()
        accumulate(step, first, second, t_out_ref, acc_ref)
    x_out_here()
    plus_gone = fetch(plus_ref, plus_hbm, sems.at[4])
    finish(x_out_ref, acc_ref, out_ref, out_hbm, out_sems)
    plus_gone()


def sigma_kernel(*refs):
    x_in_ref, t_in_ref, *tables_hbm = refs[:4]
    in_ref, base_hbm, pot_ref, plus_hbm, table_hbm, out_ref, table_ref = refs[4:11]
    (t_out_ref, x_out_ref), refs = refs[11:13], refs[13:]
    base_ref, plus_ref, left_ref, acc_ref, sems = refs
    fields_here = [
        fetch(plus_hbm, plus_ref, sems.at[3]),
        fetch(base_hbm.at[pl.ds(0, 1)], base_ref, sems.at[4]),
    ]
    t_out_here = fetch(tables_hbm[0], t_out_ref, sems.at[6])
    x_out_here = fetch(tables_hbm[1], x_out_ref, sems.at[0])
    table_here = fetch(table_hbm, table_ref, sems.at[1])

    for slab in range(2):
        high, low = halves(gather_slab(in_ref, slab))
        result = dot3(x_in_ref[0], x_in_ref[1], high, low)
        to_left(result, pl.ds(slab * 128, 128), left_ref)

    for step in range(4):
        change = to_times(step, left_ref, t_in_ref, -1)
        if step == 0:
            for field_here in fields_here:
                field_here()
        plus = plus_ref[:, time_lanes(step, 256)]
        block = time_lanes(step, 128)
        change_real, change_imag = change[:, :128], change[:, 128:]
        plus_real, plus_imag = plus[:, :128], plus[:, 128:]
        base_real, base_imag = base_ref[0, 0, :, block], base_ref[0, 1, :, block]
        pot_real, pot_imag = pot_ref[0, 0, :, block], pot_ref[0, 1, :, block]
        real = (
            pot_real * plus_real - pot_imag * plus_imag
            + change_real * base_real - change_imag * base_imag
        )
        imag = (
            pot_real * plus_imag + pot_imag * plus_real
            + change_real * base_imag + change_imag * base_real
        )
        first, second = halves(jnp.concatenate([real, imag], axis=1))
        if step == 0:
            t_out_here()
        accumulate(step, first, second, t_out_ref, acc_ref)
    x_out_here()
    finish(x_out_ref, acc_ref, out_ref)
    table_here()


PARAMS = pltpu.CompilerParams(vmem_limit_bytes=24 * 1024 * 1024)
WORK = 3 << 31
HBM = pl.BlockSpec(memory_space=pltpu.HBM)
HERE = pl.BlockSpec(memory_space=pltpu.VMEM)
TABLE = pl.BlockSpec(memory_space=pltpu.VMEM)


def call(body, name, in_specs, out_specs, out_shape, scratch, flops, *operands):
    size = sum(operand.size * operand.dtype.itemsize for operand in operands)
    return pl.pallas_call(
        body,
        in_specs=in_specs,
        out_specs=out_specs,
        out_shape=[
            pltpu.HBM(shape, F32) if spec is HBM else jax.ShapeDtypeStruct(shape, BF16 if spec is TABLE else F32)
            for shape, spec in zip(out_shape, out_specs)
        ],
        scratch_shapes=scratch,
        compiler_params=PARAMS,
        cost_estimate=pl.CostEstimate(flops=flops, bytes_accessed=size, transcendentals=0),
        name=name,
    )(*[
        pltpu.with_memory_space_constraint(operand, pltpu.HBM) if spec is HBM else operand
        for operand, spec in zip(operands, in_specs)
    ])


def like(array):
    return pltpu.VMEM(array.shape, array.dtype)


def sems(number):
    return pltpu.SemaphoreType.DMA((number,))


SLABS = (32, 4, 2, 8, 128)
TURN = 2 * 3 * 256 * 256 * 1024


def weight_call(bubble, table):
    shape = (2, 128, NF)
    return call(
        weight_kernel, "weight", [HERE, HBM], [HERE, TABLE], [shape, table.shape], [sems(1)], TURN, bubble, table
    )


def middle_call(weight, momenta, columns, held):
    scratch = [like(columns), pltpu.VMEM((2048, 128), F32), sems(5)]
    return call(
        middle_kernel, "middle", [HERE, HBM, HERE, HERE], [HBM], [(CHIPS, 32, 128)], scratch, 2 * TURN,
        momenta, columns, weight, held,
    )[0]


def last_call(table, held):
    shape = (4, 2, 2, 128, 128)
    scratch = [pltpu.VMEM((2, 4, 2, 128, 128), F32), sems(2)]
    return call(last_kernel, "last", [HERE, HERE], [HBM], [shape], scratch, TURN, table, held)[0]


def prepare_call(pieces, tables, stay):
    shape = (pieces[0].shape[0], 2, 256, NF)
    order = jnp.asarray(t_order())
    count = len(tables)
    return call(
        functools.partial(prepare_kernel, count, stay), "prepare", [HBM] * (1 + count) + [HERE] * 8,
        [TABLE] * count + [HERE if stay else HBM], [*(table.shape for table in tables), shape],
        [like(order), sems(2 + count)] + ([] if stay else [pltpu.VMEM(shape, F32)]),
        WORK, order, *tables, *pieces,
    )


def field(arrays):
    return pltpu.VMEM((arrays, 2, 256, NF), F32)


PLUS = (256, 1024)


def chi_call(tables, held, base):
    scratch = [
        *map(like, tables[1:]), field(2), pltpu.VMEM(PLUS, F32), pltpu.VMEM(SLABS, F32),
        pltpu.VMEM((4, 512, 256), F32), pltpu.VMEM((4, 256, 256), F32), sems(5), sems(2),
    ]
    return call(
        chi_kernel, "chi", [HERE, HBM, HBM, HBM, HERE, HBM], [HBM, HBM], [SLABS, PLUS], scratch, 7 * TURN,
        *tables, held.reshape(SLABS), base,
    )


def sigma_call(tables, held, base, pot, plus, table):
    scratch = [
        *map(like, tables[2:]), field(1), pltpu.VMEM(PLUS, F32),
        pltpu.VMEM((4, 256, 256), F32), pltpu.VMEM((4, 256, 256), F32), sems(7),
    ]
    return call(
        sigma_kernel, "sigma", [HERE, HERE, HBM, HBM, HERE, HBM, HERE, HBM, HBM], [HERE, TABLE],
        [SLABS, table.shape], scratch, 4 * TURN, *tables, held.reshape(SLABS), base, pot, plus, table,
    )


def exchange(source):
    source = source.reshape(128, 16, 128)
    return lax.all_to_all(source, BOTH, split_axis=0, concat_axis=0, tiled=True)


def views(arrays):
    return [
        array.reshape(32, 2, 4, 4, 128).transpose(0, 1, 3, 2, 4).reshape(64, 4, 4, 1, 128)
        for array in arrays
    ]


def pieces_of(packed):
    return [piece.reshape(-1, 256, 128) for piece in packed]


def pack(array):
    shape = (1, 64, 4, 1, 128)
    return pieces_of(
        call(pack_kernel, "pack", [HBM], [HERE] * 4, [shape] * 4, [sems(4)], 1 << 20, *views([array]))
    )


def begin(arrays, table, green):
    shape = (2, 64, 4, 1, 128)
    scratch = [
        like(table), pltpu.VMEM((2, 4, 2, 128, 128), F32), pltpu.VMEM((2048, 128), F32), sems(8), sems(5)
    ]
    *packed, sent = call(
        begin_kernel, "begin", [HBM] * 4, [HERE] * 4 + [HBM], [shape] * 4 + [(CHIPS, 32, 128)],
        scratch, TURN, *views(arrays), table, green,
    )
    return pieces_of(packed), sent


def send(rows):
    return [rows[0]] + [lax.ppermute(rows[shift], BOTH, routes(shift)) for shift in (1, 2, 3)]


def both_cores(own):
    return own + [lax.ppermute(piece, "freq", [(f, f ^ 1) for f in range(4)]) for piece in own]


def local(green_tangent, green_plus, green_mirror, potential, bubble):
    columns, momenta = jnp.asarray(y_to_columns()), jnp.asarray(y_to_momenta())
    x_table, back = jnp.asarray(split(x_in(1))), jnp.asarray(x_out())
    packed, sent = begin([green_plus, green_mirror], columns, green_tangent)
    x_here, base = prepare_call(both_cores(send(packed)), [x_table], False)
    potential, sent = lax.optimization_barrier((potential, sent))
    held = exchange(sent)
    tables = (x_here, jnp.asarray(t_in(FERMI, -1)), jnp.asarray(t_out(BOSE, 1)), back)
    sent, plus = chi_call(tables, held, base)
    potential, bubble, sent = lax.optimization_barrier((potential, bubble, sent))
    own = send(pack(potential))
    weight, momenta_here = weight_call(bubble, momenta)
    held = exchange(sent).reshape(2048, 128)
    sent = middle_call(weight, momenta_here, columns, held)
    own, sent = lax.optimization_barrier((own, sent))
    t_table = jnp.asarray(t_in(BOSE, -1))
    x_here, t_here, pot = prepare_call(both_cores(own), [x_table, t_table], True)
    held = exchange(sent)
    tables = (x_here, t_here, jnp.asarray(t_out(FERMI, 1)), back)
    sent, momenta_here = sigma_call(tables, held, base, pot, plus, momenta)
    held = exchange(sent).reshape(2048, 128)
    return last_call(momenta_here, held)


def solution(mesh):
    in_specs = (
        P("site", None, None, None, "freq"),
        P("freq", None, "site", None),
        P("freq", None, "site", None),
        P("freq", None, "site", None),
        P("site", None, None, "freq"),
    )
    out_specs = P("site", None, None, None, "freq")
    return jax.shard_map(local, mesh=mesh, in_specs=in_specs, out_specs=out_specs, check_vma=False)
```
